512 devices in a mesh: tile: 16 (over y, x_hi, core), mode: 32 (over x_lo, z).
Axes of the slice: x: 4 (x_hi: 2, x_lo: 2; x = x_hi * 2 + x_lo), y: 4, z: 16, core: 2. Of those that a mesh axis runs over, the one named last changes fastest.
Arguments:
- object_field: float32 [2, 8192, 512], P(None, ('tile', 'mode')), may hold values from -5 to 5
- probe_modes: float32 [32, 2, 256, 256], P('mode'), may hold values from -4 to 4
- measured_amplitude: float32 [16, 8, 256, 256], P('tile'), may hold values from 1 to 16
- row_offsets: int32 [16, 8], P('tile'), may hold values from 0 to 511
- col_offsets: int32 [16, 8], P('tile'), may hold values from 0 to 256
- position_counts: int32 [16], replicated, may hold values from 1 to 8, 96 in all
Outputs:
- updated_object: float32 [2, 8192, 512], P(None, ('tile', 'mode'))
The draws below stay inside these ranges and needn't reach their ends.
Inputs may be any that keep to these rules, and one draw needn't show every extreme that they name: Tile t uses its first position_counts[t] slots; some tile uses all 8.
All inputs are finite; a program needn't handle non-finite values.
Results may differ from the reference program's by a relative error of at most 0.0021.
Values may be sent and summed in bfloat16 or wider, within the bound.
No kernel may reach another device: no remote copies, remote signals or barrier semaphores. Data moves between devices by JAX's collectives and lax.ppermute only.
A program may use at most 64 MiB of HBM per device.

```python
import math
import jax
import jax.numpy as jnp
import numpy as np
from jax import lax

WIN = 256
TILE = 512
CAP = 8
TILES = 16
MODES = 32
N_TILE = 16


def draw_probe_modes(key, part):
    key = jax.random.fold_in(key, 11)
    ranks = jnp.arange(MODES, dtype=jnp.float32) / float(MODES - 1)
    weights = jnp.exp(ranks * math.log(16.0))
    scales = 0.5 * math.sqrt(MODES) * weights / jnp.sqrt(jnp.sum(weights * weights))
    base = jax.random.normal(key, (MODES, 2, WIN, WIN), jnp.float32)
    return jnp.clip(base * scales[:, None, None, None], -4.0, 4.0)


def set_ends(drawn, stream_key, low, top_value):
    dims = drawn.shape
    index_at = [jax.random.randint(jax.random.fold_in(stream_key, axis), (), 0, dims[axis]) for axis in range(len(dims))]
    drawn = drawn.at[tuple(index_at)].set(low)
    longest = dims.index(max(dims))
    index_at[longest] = (index_at[longest] + 1) % dims[longest]
    return drawn.at[tuple(index_at)].set(top_value)


def steps_of(stream_key, extent, shards, least, top_value):
    level = 1.0
    for dim, shards_of in shards:
        steps = jax.random.uniform(jax.random.fold_in(jax.random.fold_in(stream_key, 6), dim), (shards_of,), jnp.float32, least / len(shards), top_value / len(shards))
        level = level * jnp.repeat(jnp.exp(steps), extent[dim] // shards_of).reshape((-1,) + (1,) * (len(extent) - 1 - dim))
    return level


def length_profile(count, total, most, slope):
    weights = [(1 << 20) // math.isqrt(standing ** slope) + 1 for standing in range(2, count + 1)]
    surplus, counts = total - most - (count - 1), [1] * (count - 1)
    while surplus > 0:
        candidates = [i for i in range(count - 1) if counts[i] < most]
        mass, remaining = sum([weights[i] for i in candidates]), surplus
        for i in candidates:
            more = min(most - counts[i], max(1, remaining * weights[i] // mass), surplus)
            counts[i] = counts[i] + more
            surplus = surplus - more
    return np.array([most] + counts)


def ragged_sizes(rng, count, total, reach, skew):
    if count == 2:
        one = jax.random.randint(rng, (), max(1, total - reach), min(reach, total - 1) + 1)
        return jnp.stack([one, total - one])
    tallies = jnp.asarray(length_profile(count, total, reach, skew), jnp.int32)
    couples = (count - 1) // 2
    donor, receiver = tallies[1:1 + 2 * couples:2], tallies[2:2 + 2 * couples:2]
    slack = jnp.minimum(donor - 1, reach - receiver)
    passed = jax.random.randint(jax.random.fold_in(rng, 1), (couples,), 0, 1 << 20) % (slack + 1)
    tallies = tallies.at[1:1 + 2 * couples:2].set(donor - passed).at[2:2 + 2 * couples:2].set(receiver + passed)
    return tallies[jax.random.permutation(jax.random.fold_in(rng, 2), count)]


def gaussian(key, shape, deviation, bound, cuts=(), held_as=jnp.bfloat16):
    entries = deviation * jax.random.normal(key, shape, jnp.float32)
    if cuts:
        entries = entries * steps_of(key, shape, cuts, -0.22, 0.18)
    return jnp.clip(entries, -bound, bound).astype(held_as)


def setup_inputs(seed: int = 0) -> dict:
    seeds = jax.random.split(jax.random.key(seed), 7)
    return {
        "object_field": gaussian(seeds[0], (2, TILES * TILE, TILE), 0.7, 5.0, ((1, 512),), jnp.float32),
        "probe_modes": draw_probe_modes(jax.random.fold_in(seeds[6], 71), 0),
        "measured_amplitude": jnp.clip(jnp.exp(math.log(16.0) - 2.7725887 * jax.random.uniform(seeds[2], (TILES, CAP, WIN, WIN), jnp.float32) ** steps_of(seeds[2], (TILES, CAP, WIN, WIN), ((0, 16),), -0.2, 0.2)), 1.0, 16.0),
        "row_offsets": set_ends(jax.random.randint(seeds[3], (TILES, CAP), 0, TILE), jax.random.fold_in(seeds[3], 1), 0, TILE - 1).astype(jnp.int32),
        "col_offsets": set_ends(jax.random.randint(seeds[4], (TILES, CAP), 0, TILE - WIN + 1), jax.random.fold_in(seeds[4], 1), 0, TILE - WIN).astype(jnp.int32),
        "position_counts": ragged_sizes(seeds[5], TILES, N_TILE * CAP * 3 // 4, CAP, 2).astype(jnp.int32),
    }


step_size = 0.05

def dft_tables(length):
    freqs = jnp.arange(length, dtype=jnp.int32)
    turns = freqs[:, None] * freqs[None, :] % length
    phase = turns.astype(jnp.float32) * (2.0 * math.pi / length)
    norm_scale = 1.0 / math.sqrt(length)
    return ((jnp.cos(phase) * norm_scale).astype(jnp.bfloat16), (-jnp.sin(phase) * norm_scale).astype(jnp.bfloat16))

def right_product(real_in, imag_in, cos_table, sin_table):

    def prod(left_side, right_side):
        return jnp.einsum('mij,jk->mik', left_side.astype(jnp.float32), right_side.astype(jnp.float32))
    return (prod(real_in, cos_table) - prod(imag_in, sin_table), prod(real_in, sin_table) + prod(imag_in, cos_table))

def left_product(real_in, imag_in, cos_table, sin_table):

    def prod(left_side, right_side):
        return jnp.einsum('ki,mij->mkj', left_side.astype(jnp.float32), right_side.astype(jnp.float32))
    return (prod(cos_table, real_in) - prod(sin_table, imag_in), prod(sin_table, real_in) + prod(cos_table, imag_in))

def reference(object_field, probe_modes, measured_amplitude, row_offsets, col_offsets, position_counts):
    cos_table, sin_table = dft_tables(WIN)
    back_sin = -sin_table
    total_rows = TILES * TILE
    half_object = object_field.astype(jnp.bfloat16)
    padded = jnp.concatenate([half_object, jnp.zeros((2, WIN, TILE), jnp.bfloat16)], axis=1)
    tile_ids = jnp.repeat(jnp.arange(TILES, dtype=jnp.int32), CAP)
    row_starts = (tile_ids * TILE + row_offsets.reshape(-1)).astype(jnp.int32)
    col_starts = col_offsets.reshape(-1).astype(jnp.int32)
    alive_mask = (jnp.arange(CAP, dtype=jnp.int32)[None, :] < position_counts[:, None]).astype(jnp.float32).reshape(-1)
    amplitudes = measured_amplitude.reshape(TILES * CAP, WIN, WIN)
    zero_index = jnp.zeros((), jnp.int32)

    def one_position(gradient, scanned):
        row_start, col_start, amplitude, alive = scanned
        patch = lax.dynamic_slice(padded, (zero_index, row_start, col_start), (2, WIN, WIN)).astype(jnp.float32)
        exit_real = (probe_modes[:, 0] * patch[0] - probe_modes[:, 1] * patch[1]).astype(jnp.bfloat16)
        exit_imag = (probe_modes[:, 0] * patch[1] + probe_modes[:, 1] * patch[0]).astype(jnp.bfloat16)
        half_real, half_imag = right_product(exit_real, exit_imag, cos_table, sin_table)
        spec_real, spec_imag = left_product(half_real.astype(jnp.bfloat16), half_imag.astype(jnp.bfloat16), cos_table, sin_table)
        intensity = lax.optimization_barrier(jnp.sum(spec_real * spec_real + spec_imag * spec_imag, axis=0))
        factor = alive * (1.0 - amplitude / jnp.sqrt(intensity + 1.0))
        wave_real = (spec_real * factor).astype(jnp.bfloat16)
        wave_imag = (spec_imag * factor).astype(jnp.bfloat16)
        back_real, back_imag = right_product(wave_real, wave_imag, cos_table, back_sin)
        grad_real, grad_imag = left_product(back_real.astype(jnp.bfloat16), back_imag.astype(jnp.bfloat16), cos_table, back_sin)
        term_real = lax.optimization_barrier(jnp.sum(probe_modes[:, 0] * grad_real + probe_modes[:, 1] * grad_imag, axis=0))
        term_imag = lax.optimization_barrier(jnp.sum(probe_modes[:, 0] * grad_imag - probe_modes[:, 1] * grad_real, axis=0))
        term = jnp.stack([term_real, term_imag])
        current = lax.dynamic_slice(gradient, (zero_index, row_start, col_start), (2, WIN, WIN))
        gradient = lax.dynamic_update_slice(gradient, current + term, (zero_index, row_start, col_start))
        return (gradient, None)
    start_grad = jnp.zeros((2, total_rows + WIN, TILE), jnp.float32)
    gradient, unused = lax.scan(one_position, start_grad, (row_starts, col_starts, amplitudes, alive_mask))
    return object_field - step_size * gradient[:, :total_rows]
```

```python
import functools
import math

import jax
import jax.numpy as jnp
import numpy as np
from jax import lax
from jax.experimental import pallas as pl
from jax.experimental.pallas import tpu as pltpu
from jax.sharding import Mesh, PartitionSpec as P

step_size = 0.05
f32 = jnp.float32
bf16 = jnp.bfloat16
TILE_AXES = ("y", "xh", "c")
SPARE = 16
VMEM_LIMIT = 48 * 1024 * 1024


def dft_blocks(length):
    freqs = np.arange(length, dtype=np.int32)
    turns = freqs[:, None] * freqs[None, :] % length
    phase = turns.astype(np.float32) * np.float32(2.0 * math.pi / length)
    norm_scale = np.float32(1.0 / math.sqrt(length))
    cos_table = (np.cos(phase) * norm_scale).astype(jnp.bfloat16)
    sin_table = (-np.sin(phase) * norm_scale).astype(jnp.bfloat16)
    right = np.block([[cos_table, sin_table], [-sin_table, cos_table]])
    left = np.block([[cos_table, -sin_table], [sin_table, cos_table]])
    return right, left


def dot(left_side, right_side):
    return jnp.dot(left_side, right_side, preferred_element_type=f32)


def side_by_side(stacked):
    size = stacked.shape[0] // 2
    return jnp.concatenate([stacked[:size], stacked[size:]], axis=1)


def on_top(beside):
    size = beside.shape[1] // 2
    return jnp.concatenate([beside[:, :size], beside[:, size:]], axis=0)


def forward_kernel(
    rows_ref, cols_ref, lane_ref, mine_ref, other_ref, below_ref, probe_ref, right_ref, left_ref,
    spec_ref, power_ref, extended,
):
    slot = pl.program_id(0)
    chunks, _, chunk_rows, width = mine_ref.shape
    modes, _, window, _ = probe_ref.shape
    half = chunks * chunk_rows
    lane = lane_ref[0]

    @pl.when(slot == 0)
    def _():
        extended[:, pl.ds(3 * half, SPARE), :] = jnp.zeros((2, SPARE, width), f32)
        for source, base in (
            (mine_ref, lane * half), (other_ref, (1 - lane) * half), (below_ref, 2 * half)
        ):
            for chunk in range(chunks):
                start = base + chunk * chunk_rows
                if not isinstance(start, int):
                    start = pl.multiple_of(start, chunk_rows)
                for part in range(2):
                    extended[part, pl.ds(start, chunk_rows), :] = source[chunk, part].astype(f32)

    place = lane * pl.num_programs(0) + slot
    row_start = rows_ref[place]
    col_start = cols_ref[place]
    source_col = lax.broadcasted_iota(jnp.int32, (width, window), 0)
    target_col = lax.broadcasted_iota(jnp.int32, (width, window), 1)
    pick = (source_col == target_col + col_start).astype(f32).astype(bf16)
    aligned = pl.multiple_of(row_start // 8 * 8, 8)
    taken = window + SPARE
    back_turn = (taken - row_start % 8) % taken

    def cut_patch(part):
        columns = dot(extended[part, pl.ds(aligned, taken), :].astype(bf16), pick)
        return pltpu.roll(columns, back_turn, 0)[:window]

    patch_real, patch_imag = cut_patch(0), cut_patch(1)
    power = None
    for mode in range(modes):
        probe_real, probe_imag = probe_ref[mode, 0], probe_ref[mode, 1]
        exit_real = (probe_real * patch_real - probe_imag * patch_imag).astype(bf16)
        exit_imag = (probe_real * patch_imag + probe_imag * patch_real).astype(bf16)
        half_spectrum = dot(jnp.concatenate([exit_real, exit_imag], axis=1), right_ref[...])
        spectrum = dot(left_ref[...], on_top(half_spectrum.astype(bf16)))
        spec_ref[0, mode] = spectrum
        squares = spectrum * spectrum
        term = squares[:window] + squares[window:]
        power = term if power is None else power + term
    power_ref[0] = power.astype(bf16)


def backward_kernel(
    rows_ref, cols_ref, lane_ref, spec_ref, factor_ref, probe_ref, right_ref, left_ref,
    mine_ref, other_ref, below_ref, gradient,
):
    slot = pl.program_id(0)
    chunks, _, chunk_rows, width = mine_ref.shape
    modes, _, window, _ = probe_ref.shape
    half = chunks * chunk_rows
    lane = lane_ref[0]

    @pl.when(slot == 0)
    def _():
        gradient[...] = jnp.zeros_like(gradient)

    factor = factor_ref[0].astype(f32)
    factor = jnp.concatenate([factor, factor], axis=0)
    sum_real, sum_imag = None, None
    for mode in range(modes):
        wave = (spec_ref[0, mode] * factor).astype(bf16)
        back_half = dot(side_by_side(wave), left_ref[...])
        back_wave = dot(right_ref[...], on_top(back_half.astype(bf16)))
        back_real, back_imag = back_wave[:window], back_wave[window:]
        probe_real, probe_imag = probe_ref[mode, 0], probe_ref[mode, 1]
        term_real = probe_real * back_real + probe_imag * back_imag
        term_imag = probe_real * back_imag - probe_imag * back_real
        sum_real = term_real if sum_real is None else sum_real + term_real
        sum_imag = term_imag if sum_imag is None else sum_imag + term_imag

    place = lane * pl.num_programs(0) + slot
    row_start = rows_ref[place]
    col_start = cols_ref[place]
    source_col = lax.broadcasted_iota(jnp.int32, (window, width), 0)
    target_col = lax.broadcasted_iota(jnp.int32, (window, width), 1)
    spread = (target_col == source_col + col_start).astype(f32).astype(bf16)
    aligned = pl.multiple_of(row_start // 8 * 8, 8)
    spare = jnp.zeros((SPARE, window), f32)
    for part, term in enumerate((sum_real, sum_imag)):
        moved = pltpu.roll(jnp.concatenate([term, spare], axis=0), row_start % 8, 0)
        high = moved.astype(bf16)
        low = (moved - high.astype(f32)).astype(bf16)
        at_rows = pl.ds(aligned, window + SPARE)
        gradient[part, at_rows, :] = gradient[part, at_rows, :] + (dot(high, spread) + dot(low, spread))

    @pl.when(slot == pl.num_programs(0) - 1)
    def _():
        for target, base in (
            (mine_ref, lane * half), (other_ref, (1 - lane) * half), (below_ref, 2 * half)
        ):
            for chunk in range(chunks):
                start = base + chunk * chunk_rows
                if not isinstance(start, int):
                    start = pl.multiple_of(start, chunk_rows)
                for part in range(2):
                    target[chunk, part] = gradient[part, pl.ds(start, chunk_rows), :].astype(target.dtype)


def whole(shape):
    return pl.BlockSpec(shape, lambda slot, *_: (0,) * len(shape))


def per_slot(shape):
    return pl.BlockSpec((1,) + shape, lambda slot, *_: (slot,) + (0,) * len(shape))


def to_all(block, axis):
    copies = jnp.broadcast_to(block[None], (lax.axis_size(axis),) + block.shape)
    return lax.all_to_all(copies, axis, 0, 0, tiled=True)


def on_device(
    object_field, probe_modes, measured_amplitude, row_offsets, col_offsets, position_counts
):
    window = probe_modes.shape[-1]
    slots = row_offsets.shape[1]
    width = object_field.shape[2]
    depth = lax.axis_size("z")
    tiles = lax.axis_size(TILE_AXES)
    chunk_rows = object_field.shape[1]
    lane = lax.axis_index("xl")
    here = lax.axis_index("z")
    right, left = (jnp.asarray(table) for table in dft_blocks(window))
    own_slots = slots // lax.axis_size("xl")
    swap = [(0, 1), (1, 0)]
    upwards = [(i, i - 1) for i in range(1, tiles)]
    downwards = [(i - 1, i) for i in range(1, tiles)]

    other_probe = lax.ppermute(probe_modes, "xl", swap)
    mine = to_all(object_field.astype(bf16), "z")
    other = lax.ppermute(mine, "xl", swap)
    top = jnp.where(lane == 0, mine, other)
    below = lax.ppermute(top, TILE_AXES, upwards)
    probes = jnp.concatenate([probe_modes, other_probe], axis=0)

    scalars = (row_offsets[0], col_offsets[0], lane.astype(jnp.int32)[None])
    chunked = (depth, 2, chunk_rows, width)
    modes = probes.shape[0]
    product_flops = own_slots * modes * 2 * 2 * (2 * window) ** 2 * window
    spectrum, power = pl.pallas_call(
        forward_kernel,
        grid_spec=pltpu.PrefetchScalarGridSpec(
            num_scalar_prefetch=3,
            grid=(own_slots,),
            in_specs=[whole(chunked)] * 3
            + [whole(probes.shape), whole(right.shape), whole(left.shape)],
            out_specs=[per_slot((modes, 2 * window, window)), per_slot((window, window))],
            scratch_shapes=[pltpu.VMEM((2, 3 * depth * chunk_rows + SPARE, width), f32)],
        ),
        out_shape=[
            jax.ShapeDtypeStruct((own_slots, modes, 2 * window, window), f32),
            jax.ShapeDtypeStruct((own_slots, window, window), bf16),
        ],
        compiler_params=pltpu.CompilerParams(vmem_limit_bytes=VMEM_LIMIT),
        cost_estimate=pl.CostEstimate(
            flops=product_flops, bytes_accessed=8 * 1024 * 1024, transcendentals=0
        ),
        name="forward",
    )(*scalars, mine, other, below, probes, right, left)

    pieces = lax.all_to_all(
        power.reshape(depth, own_slots * window // depth, window), "z", 0, 0, tiled=True
    )
    intensity = jnp.sum(pieces.astype(f32), axis=0)
    piece_rows = intensity.shape[0]
    per_window = window // piece_rows
    slot = lane * own_slots + here // per_window
    amplitude = lax.dynamic_slice(
        measured_amplitude[0],
        (slot, here % per_window * piece_rows, jnp.zeros((), slot.dtype)),
        (1, piece_rows, window),
    )[0]
    alive = (slot < position_counts[lax.axis_index(TILE_AXES)]).astype(f32)
    factor_piece = (alive * (1.0 - amplitude / jnp.sqrt(intensity + 1.0))).astype(bf16)
    factor = to_all(factor_piece, "z").reshape(own_slots, window, window)

    kept, sent, beneath = pl.pallas_call(
        backward_kernel,
        grid_spec=pltpu.PrefetchScalarGridSpec(
            num_scalar_prefetch=3,
            grid=(own_slots,),
            in_specs=[per_slot((modes, 2 * window, window)), per_slot((window, window))]
            + [whole(probes.shape), whole(right.shape), whole(left.shape)],
            out_specs=[whole(chunked)] * 3,
            scratch_shapes=[pltpu.VMEM((2, 3 * depth * chunk_rows + SPARE, width), f32)],
        ),
        out_shape=[
            jax.ShapeDtypeStruct(chunked, f32),
            jax.ShapeDtypeStruct(chunked, f32),
            jax.ShapeDtypeStruct(chunked, bf16),
        ],
        compiler_params=pltpu.CompilerParams(vmem_limit_bytes=VMEM_LIMIT),
        cost_estimate=pl.CostEstimate(
            flops=product_flops, bytes_accessed=8 * 1024 * 1024, transcendentals=0
        ),
        name="backward",
    )(*scalars, spectrum, factor, probes, right, left)

    from_above = lax.ppermute(beneath, TILE_AXES, downwards).astype(f32)
    zero = jnp.zeros((), f32)
    outgoing = (sent + jnp.where(lane == 1, from_above, zero)).astype(bf16)
    incoming = lax.ppermute(outgoing, "xl", swap).astype(f32)
    own_half = kept + jnp.where(lane == 0, from_above, zero) + incoming
    terms = lax.all_to_all(own_half.astype(bf16), "z", 0, 0, tiled=True)
    return object_field - step_size * jnp.sum(terms.astype(f32), axis=0)


def solution(mesh):
    tiles, modes = mesh.devices.shape
    parts = Mesh(mesh.devices.reshape(tiles // 4, 2, 2, 2, modes // 2), TILE_AXES + ("xl", "z"))
    placed = (
        P(None, TILE_AXES + ("xl", "z"), None),
        P(("xl", "z"), None, None, None),
        P(TILE_AXES, None, None, None),
        P(TILE_AXES, None),
        P(TILE_AXES, None),
        P(),
    )
    return jax.shard_map(
        on_device,
        mesh=parts,
        in_specs=placed,
        out_specs=P(None, TILE_AXES + ("xl", "z"), None),
        check_vma=False,
    )
```

```python
import math

import jax
import jax.numpy as jnp
import numpy as np
from jax import lax
from jax.experimental import pallas as pl
from jax.experimental.pallas import tpu as pltpu
from jax.sharding import Mesh, PartitionSpec as P

step_size = 0.05
f32 = jnp.float32
bf16 = jnp.bfloat16
TILE_AXES = ("y", "xh", "c")
DEPTH_AXES = ("zq", "zr")
VMEM_LIMIT = 48 * 1024 * 1024


def dft_blocks(length):
    freqs = np.arange(length, dtype=np.int32)
    turns = freqs[:, None] * freqs[None, :] % length
    phase = turns.astype(np.float32) * np.float32(2.0 * math.pi / length)
    norm_scale = np.float32(1.0 / math.sqrt(length))
    cos_table = (np.cos(phase) * norm_scale).astype(jnp.bfloat16)
    sin_table = (-np.sin(phase) * norm_scale).astype(jnp.bfloat16)
    right = np.block([[cos_table, sin_table], [-sin_table, cos_table]])
    left = np.block([[cos_table, -sin_table], [sin_table, cos_table]])
    return right, left


def dot(left_side, right_side):
    return jnp.dot(left_side, right_side, preferred_element_type=f32)


def on_top(beside):
    size = beside.shape[1] // 2
    return jnp.concatenate([beside[:, :size], beside[:, size:]], axis=0)


def one_hot(rows, columns, offset):
    row = lax.broadcasted_iota(jnp.int32, (rows, columns), 0)
    column = lax.broadcasted_iota(jnp.int32, (rows, columns), 1)
    return (column == row + offset).astype(f32).astype(bf16)


def one_hot_down(rows, columns, offset):
    row = lax.broadcasted_iota(jnp.int32, (rows, columns), 0)
    column = lax.broadcasted_iota(jnp.int32, (rows, columns), 1)
    return (row == column + offset).astype(f32).astype(bf16)


def cut_kernel(
    meta_ref, cols_ref, above_ref, half_ref, pair_ref, near_ref, far_ref, last_ref,
    own_ref, partner_ref, upper_ref, lower_ref, probe_ref,
):
    chunks, _, _, width = half_ref.shape
    window = own_ref.shape[-1]
    slots = cols_ref.shape[0]
    lane, quarter = meta_ref[0], meta_ref[1]
    quarters = slots // 2
    starts = (
        cols_ref[lane * quarters + quarter],
        cols_ref[(1 - lane) * quarters + quarter],
        above_ref[slots + quarter],
        above_ref[slots + quarters + quarter],
    )
    for part in range(2):
        rows = jnp.concatenate([half_ref[chunk, part] for chunk in range(chunks)], axis=0)
        for target, start in zip((own_ref, partner_ref, upper_ref, lower_ref), starts):
            target[part] = dot(rows, one_hot_down(width, window, start)).astype(bf16)
    for index, source in enumerate((pair_ref, near_ref, far_ref, last_ref)):
        probe_ref[index] = source[...]


def full_probe(here_ref, there_ref, core, mode):
    def rows(part):
        here, there = here_ref[0, mode, part].astype(f32), there_ref[0, mode, part].astype(f32)
        first = jnp.where(core == 0, here, there)
        second = jnp.where(core == 0, there, here)
        return jnp.concatenate([first, second], axis=0)

    return rows(0), rows(1)


def forward_kernel(
    meta_ref, rows_ref, own_ref, other_ref, below0_ref, below1_ref, here_ref, there_ref,
    right_ref, left_ref, spec_ref, power_ref, patch, total,
):
    step = pl.program_id(0)
    lane, quarter, core = meta_ref[0], meta_ref[1], meta_ref[2]
    window = own_ref.shape[-1]
    height = own_ref.shape[1]
    row_start = rows_ref[lane * (rows_ref.shape[0] // 2) + quarter]

    @pl.when(step == 0)
    def _():
        pick = jnp.concatenate(
            [
                one_hot(window, height, row_start - lane * height),
                one_hot(window, height, row_start - (1 - lane) * height),
                one_hot(window, height, row_start - 2 * height),
            ],
            axis=1,
        )
        for part in range(2):
            below = below0_ref[part] + below1_ref[part]
            patch[part] = dot(pick, jnp.concatenate([own_ref[part], other_ref[part], below], axis=0))
        total[...] = jnp.zeros_like(total)

    for mode in range(here_ref.shape[1]):
        probe_real, probe_imag = full_probe(here_ref, there_ref, core, mode)
        exit_real = (probe_real * patch[0] - probe_imag * patch[1]).astype(bf16)
        exit_imag = (probe_real * patch[1] + probe_imag * patch[0]).astype(bf16)
        half_spectrum = dot(jnp.concatenate([exit_real, exit_imag], axis=1), right_ref[...])
        spectrum = dot(left_ref[...], on_top(half_spectrum.astype(bf16)))
        spec_ref[0, mode] = spectrum
        squares = spectrum * spectrum
        total[...] = total[...] + (squares[:window] + squares[window:])

    @pl.when(step == pl.num_programs(0) - 1)
    def _():
        power_ref[...] = total[...].astype(bf16)


def backward_kernel(
    meta_ref, spec_ref, powers_ref, amplitude_ref, here_ref, there_ref, right_ref, left_ref,
    window_ref, factor, sums,
):
    step = pl.program_id(0)
    core, alive = meta_ref[2], meta_ref[3]
    window = window_ref.shape[-1]

    @pl.when(step == 0)
    def _():
        intensity = powers_ref[0].astype(f32)
        for member in range(1, powers_ref.shape[0]):
            intensity = intensity + powers_ref[member].astype(f32)
        correction = 1.0 - amplitude_ref[0] / jnp.sqrt(intensity + 1.0)
        factor[...] = alive.astype(f32) * correction
        sums[...] = jnp.zeros_like(sums)

    for mode in range(here_ref.shape[1]):
        wave_real = (spec_ref[0, mode, :window] * factor[...]).astype(bf16)
        wave_imag = (spec_ref[0, mode, window:] * factor[...]).astype(bf16)
        back_half = dot(jnp.concatenate([wave_real, wave_imag], axis=1), left_ref[...])
        back_wave = dot(right_ref[...], on_top(back_half.astype(bf16)))
        back_real, back_imag = back_wave[:window], back_wave[window:]
        probe_real, probe_imag = full_probe(here_ref, there_ref, core, mode)
        sums[0] = sums[0] + (probe_real * back_real + probe_imag * back_imag)
        sums[1] = sums[1] + (probe_real * back_imag - probe_imag * back_real)

    @pl.when(step == pl.num_programs(0) - 1)
    def _():
        window_ref[...] = sums[...].astype(bf16)


def place_kernel(
    meta_ref, rows_ref, cols_ref, above_ref, own_ref, partner_ref, upper_ref, lower_ref, half_ref
):
    chunks, _, chunk_rows, width = half_ref.shape
    height = chunks * chunk_rows
    window = own_ref.shape[-1]
    slots = rows_ref.shape[0]
    quarters = slots // 2
    lane, quarter = meta_ref[0], meta_ref[1]
    mine, partners = lane * quarters + quarter, (1 - lane) * quarters + quarter
    first, second = quarter, quarters + quarter
    row_starts = (
        rows_ref[mine] - lane * height,
        rows_ref[partners] - lane * height,
        above_ref[first] - 2 * height,
        above_ref[second] - 2 * height,
    )
    col_starts = (
        cols_ref[mine], cols_ref[partners], above_ref[slots + first], above_ref[slots + second]
    )
    spread = jnp.concatenate([one_hot(window, width, start) for start in col_starts], axis=0)
    sources = (own_ref, partner_ref, upper_ref, lower_ref)
    shifts = [one_hot_down(height, window, start) for start in row_starts]
    for part in range(2):
        moved = [dot(shift, source[part]).astype(bf16) for shift, source in zip(shifts, sources)]
        placed = dot(jnp.concatenate(moved, axis=1), spread).astype(bf16)
        for chunk in range(chunks):
            half_ref[chunk, part] = placed[chunk * chunk_rows : (chunk + 1) * chunk_rows]


def whole(shape):
    return pl.BlockSpec(shape, lambda step, *_: (0,) * len(shape))


def per_step(shape):
    return pl.BlockSpec((1,) + shape, lambda step, *_: (step,) + (0,) * len(shape))


def call(kernel, name, scalars, operands, in_specs, results, out_specs, steps=1, scratch=(), flops=0):
    return pl.pallas_call(
        kernel,
        grid_spec=pltpu.PrefetchScalarGridSpec(
            num_scalar_prefetch=len(scalars),
            grid=(steps,),
            in_specs=in_specs,
            out_specs=out_specs,
            scratch_shapes=scratch,
        ),
        out_shape=results,
        compiler_params=pltpu.CompilerParams(vmem_limit_bytes=VMEM_LIMIT),
        cost_estimate=pl.CostEstimate(
            flops=flops, bytes_accessed=4 * 1024 * 1024, transcendentals=0
        ),
        name=name,
    )(*scalars, *operands)


def to_all(block, axis):
    size = lax.axis_size(axis)
    return lax.all_to_all(jnp.broadcast_to(block[None], (size,) + block.shape), axis, 0, 0, tiled=True)


def on_device(
    object_field, probe_modes, measured_amplitude, row_offsets, col_offsets, position_counts
):
    window = probe_modes.shape[-1]
    slots = row_offsets.shape[1]
    width = object_field.shape[2]
    chunk_rows = object_field.shape[1]
    depth = lax.axis_size(DEPTH_AXES)
    quarters = lax.axis_size("zq")
    tiles = lax.axis_size(TILE_AXES)
    lane, quarter, core = lax.axis_index("xl"), lax.axis_index("zq"), lax.axis_index("c")
    right, left = (jnp.asarray(table) for table in dft_blocks(window))
    swap = [(0, 1), (1, 0)]
    axes = TILE_AXES + ("xl",)
    up_first = [(2 * (t + 1), 2 * t) for t in range(tiles - 1)]
    up_second = [(2 * (t + 1), 2 * t + 1) for t in range(tiles - 1)]
    down_first = [(2 * t, 2 * (t + 1)) for t in range(tiles - 1)]
    down_second = [(2 * t + 1, 2 * (t + 1)) for t in range(tiles - 1)]
    downwards = [(t, t + 1) for t in range(tiles - 1)]

    count = position_counts[lax.axis_index(TILE_AXES)]
    alive = (lane * quarters + quarter < count).astype(jnp.int32)
    meta = jnp.stack([lane, quarter, core, alive]).astype(jnp.int32)
    rows, cols = row_offsets[0], col_offsets[0]
    above = lax.ppermute(jnp.concatenate([rows, cols]), TILE_AXES, downwards)

    part_rows = window // 2
    probe_part = lax.dynamic_slice_in_dim(
        probe_modes.astype(bf16), core * part_rows, part_rows, axis=2
    )
    pair = jnp.concatenate([probe_part, lax.ppermute(probe_part, "xl", swap)], axis=0)
    brought = [
        lax.ppermute(pair, "zq", [(i, (i + d) % quarters) for i in range(quarters)])
        for d in range(1, quarters)
    ]
    half = to_all(object_field.astype(bf16), DEPTH_AXES)

    patch_shape = (2, half.shape[0] * chunk_rows, window)
    window_shape = (2, window, window)
    probes_shape = (quarters,) + pair.shape
    own, partner, upper, lower, here = call(
        cut_kernel, "cut", (meta, cols, above), (half, pair, *brought),
        [whole(half.shape)] + [whole(pair.shape)] * 4,
        [jax.ShapeDtypeStruct(patch_shape, bf16)] * 4 + [jax.ShapeDtypeStruct(probes_shape, bf16)],
        [whole(patch_shape)] * 4 + [whole(probes_shape)],
    )
    there = lax.ppermute(here, "c", swap)
    other = lax.ppermute(partner, "xl", swap)
    below0 = lax.ppermute(upper, axes, up_first)
    below1 = lax.ppermute(lower, axes, up_second)

    modes = quarters * pair.shape[0]
    product_flops = modes * 2 * 2 * (2 * window) ** 2 * window
    probe_block = per_step(pair.shape)
    spec_shape = (pair.shape[0], 2 * window, window)
    spectrum, power = call(
        forward_kernel, "forward", (meta, rows),
        (own, other, below0, below1, here, there, right, left),
        [whole(patch_shape)] * 4 + [probe_block] * 2 + [whole(right.shape), whole(left.shape)],
        [
            jax.ShapeDtypeStruct((quarters,) + spec_shape, f32),
            jax.ShapeDtypeStruct((window, window), bf16),
        ],
        [per_step(spec_shape), whole((window, window))],
        steps=quarters,
        scratch=[pltpu.VMEM(window_shape, f32), pltpu.VMEM((window, window), f32)],
        flops=product_flops,
    )
    powers = lax.all_gather(power, "zr", axis=0)

    slot_block = pl.BlockSpec(
        (1, window, window), lambda step, meta_ref: (meta_ref[0] * quarters + meta_ref[1], 0, 0)
    )
    term = call(
        backward_kernel, "backward", (meta,),
        (spectrum, powers, measured_amplitude[0], here, there, right, left),
        [per_step(spec_shape), whole(powers.shape), slot_block]
        + [probe_block] * 2 + [whole(right.shape), whole(left.shape)],
        jax.ShapeDtypeStruct(window_shape, bf16),
        whole(window_shape),
        steps=quarters,
        scratch=[pltpu.VMEM((window, window), f32), pltpu.VMEM(window_shape, f32)],
        flops=product_flops,
    )

    partners = lax.ppermute(term, "xl", swap)
    above0 = lax.ppermute(term, axes, down_first)
    above1 = lax.ppermute(term, axes, down_second)
    half_sum = call(
        place_kernel, "place", (meta, rows, cols, above), (term, partners, above0, above1),
        [whole(window_shape)] * 4,
        jax.ShapeDtypeStruct(half.shape, bf16),
        whole(half.shape),
    )
    terms = lax.all_to_all(half_sum, DEPTH_AXES, 0, 0, tiled=True)
    return object_field - step_size * jnp.sum(terms.astype(f32), axis=0)


def solution(mesh):
    tiles, modes = mesh.devices.shape
    parts = Mesh(
        mesh.devices.reshape(tiles // 4, 2, 2, 2, 4, modes // 8), TILE_AXES + ("xl",) + DEPTH_AXES
    )
    tile, mode = TILE_AXES, ("xl",) + DEPTH_AXES
    placed = (
        P(None, tile + mode, None),
        P(mode, None, None, None),
        P(tile, None, None, None),
        P(tile, None),
        P(tile, None),
        P(),
    )
    return jax.shard_map(
        on_device,
        mesh=parts,
        in_specs=placed,
        out_specs=P(None, tile + mode, None),
        check_vma=False,
    )
```

```python
import math

import jax
import jax.numpy as jnp
import numpy as np
from jax import lax
from jax.experimental import pallas as pl
from jax.experimental.pallas import tpu as pltpu
from jax.sharding import Mesh, PartitionSpec as P

step_size = 0.05
f32 = jnp.float32
bf16 = jnp.bfloat16
TILE_AXES = ("y", "xh", "c")
DEPTH_AXES = ("zq", "zr")
STEPS = 2
CHUNK = 16
QUARTERS = 4
RUN = 4
VMEM_LIMIT = 48 * 1024 * 1024


def dft_blocks(length):
    freqs = np.arange(length, dtype=np.int32)
    turns = freqs[:, None] * freqs[None, :] % length
    phase = turns.astype(np.float32) * np.float32(2.0 * math.pi / length)
    norm_scale = np.float32(1.0 / math.sqrt(length))
    cos_table = (np.cos(phase) * norm_scale).astype(jnp.bfloat16)
    sin_table = (-np.sin(phase) * norm_scale).astype(jnp.bfloat16)
    right = np.block([[cos_table, sin_table], [-sin_table, cos_table]])
    left = np.block([[cos_table, -sin_table], [sin_table, cos_table]])
    return right, left


def dot(left_side, right_side):
    return jnp.dot(left_side, right_side, preferred_element_type=f32)


def on_top(beside):
    size = beside.shape[1] // 2
    return jnp.concatenate([beside[:, :size], beside[:, size:]], axis=0)


def one_hot(rows, columns, offset):
    row = lax.broadcasted_iota(jnp.int32, (rows, columns), 0)
    column = lax.broadcasted_iota(jnp.int32, (rows, columns), 1)
    return (column == row + offset).astype(f32).astype(bf16)


def one_hot_down(rows, columns, offset):
    row = lax.broadcasted_iota(jnp.int32, (rows, columns), 0)
    column = lax.broadcasted_iota(jnp.int32, (rows, columns), 1)
    return (row == column + offset).astype(f32).astype(bf16)


def first_row(row_start, member):
    return (row_start // CHUNK - member + RUN - 1) // RUN * CHUNK


def class_rows(touched, window, row_start, across):
    blocks = []
    for member in range(RUN):
        shape = (window, touched) if across else (touched, window)
        spot = lax.broadcasted_iota(jnp.int32, shape, 1 if across else 0)
        row = lax.broadcasted_iota(jnp.int32, shape, 0 if across else 1)
        chunk = (first_row(row_start, member) // CHUNK + spot // CHUNK) * RUN + member
        blocks.append((chunk * CHUNK + spot % CHUNK == row + row_start).astype(f32).astype(bf16))
    return jnp.concatenate(blocks, axis=1 if across else 0)


def cut_kernel(
    meta_ref, scan_ref, above_ref, packed_ref, own_ref, partner_ref, upper_ref, lower_ref, probe_ref
):
    chunks, _, _, width = packed_ref.shape
    window = own_ref.shape[-1]
    quarters = chunks
    slots = 2 * quarters
    lane, quarter = meta_ref[0], meta_ref[1]
    starts = (
        scan_ref[slots + lane * quarters + quarter],
        scan_ref[slots + (1 - lane) * quarters + quarter],
        above_ref[slots + quarter],
        above_ref[slots + quarters + quarter],
    )
    pick = jnp.concatenate([one_hot_down(width, window, start) for start in starts], axis=1)
    for part in range(2):
        rows = jnp.concatenate([packed_ref[chunk, part, :CHUNK] for chunk in range(chunks)], axis=0)
        columns = dot(rows, pick).astype(bf16)
        for index, target in enumerate((own_ref, partner_ref, upper_ref, lower_ref)):
            target[part] = columns[:, index * window : (index + 1) * window]
        for chunk in range(chunks):
            probe_ref[chunk, part] = packed_ref[chunk, part, CHUNK:]


def touch_kernel(
    meta_ref, scan_ref, own_ref, other_ref, below0_ref, below1_ref, touched_ref
):
    lane, quarter, member = meta_ref[0], meta_ref[1], meta_ref[5]
    height = own_ref.shape[1]
    touched = touched_ref.shape[1]
    row_start = scan_ref[lane * QUARTERS + quarter]
    first = first_row(row_start, member)
    pick = jnp.concatenate(
        [
            one_hot(touched, height, first - lane * height),
            one_hot(touched, height, first - (1 - lane) * height),
            one_hot(touched, height, first - 2 * height),
        ],
        axis=1,
    )
    for part in range(2):
        below = below0_ref[part] + below1_ref[part]
        stack = jnp.concatenate([own_ref[part], other_ref[part], below], axis=0)
        touched_ref[part] = dot(pick, stack).astype(bf16)


def full_probe(here_ref, there_ref, meta_ref, mode):
    core, up = meta_ref[2], meta_ref[6]
    count = here_ref.shape[0]
    window = here_ref.shape[-1] // 2

    def rows(part):
        pieces = []
        for row in range(count):
            place = lax.rem(up - row + count, count)
            here = here_ref[place, mode, part].astype(f32)
            there = there_ref[place, mode, part].astype(f32)
            for piece in (jnp.where(core == 0, here, there), jnp.where(core == 0, there, here)):
                pieces += [piece[:, :window], piece[:, window:]]
        return jnp.concatenate(pieces, axis=0)

    return rows(0), rows(1)


def forward_kernel(
    meta_ref, scan_ref, touched_ref, here_ref, there_ref,
    right_ref, left_ref, spec_ref, power_ref, patch, total,
):
    step = pl.program_id(0)
    lane, quarter = meta_ref[0], meta_ref[1]
    window = power_ref.shape[-1]
    row_start = scan_ref[lane * QUARTERS + quarter]

    @pl.when(step == 0)
    def _():
        pick = class_rows(touched_ref.shape[2], window, row_start, True)
        for part in range(2):
            stack = jnp.concatenate([touched_ref[member, part] for member in range(RUN)], axis=0)
            patch[part] = dot(pick, stack)
        total[...] = jnp.zeros_like(total)

    for mode in range(here_ref.shape[1]):
        probe_real, probe_imag = full_probe(here_ref, there_ref, meta_ref, mode)
        exit_real = (probe_real * patch[0] - probe_imag * patch[1]).astype(bf16)
        exit_imag = (probe_real * patch[1] + probe_imag * patch[0]).astype(bf16)
        half_spectrum = dot(jnp.concatenate([exit_real, exit_imag], axis=1), right_ref[...])
        spectrum = dot(left_ref[...], on_top(half_spectrum.astype(bf16)))
        spec_ref[0, mode] = spectrum
        squares = spectrum * spectrum
        total[...] = total[...] + (squares[:window] + squares[window:])

    @pl.when(step == pl.num_programs(0) - 1)
    def _():
        power_ref[...] = total[...].astype(bf16)


def backward_kernel(
    meta_ref, scan_ref, spec_ref, powers_ref, amplitude_ref, here_ref, there_ref, right_ref, left_ref,
    pieces_ref, factor, sums,
):
    step = pl.program_id(0)
    slot = meta_ref[0] * QUARTERS + meta_ref[1]
    alive = slot < scan_ref[4 * QUARTERS + meta_ref[3]]
    window = pieces_ref.shape[-1]

    @pl.when(step == 0)
    def _():
        intensity = powers_ref[0].astype(f32)
        for member in range(1, powers_ref.shape[0]):
            intensity = intensity + powers_ref[member].astype(f32)
        correction = 1.0 - amplitude_ref[0] / jnp.sqrt(intensity + 1.0)
        factor[...] = jnp.where(alive, correction, 0.0)
        sums[...] = jnp.zeros_like(sums)

    for mode in range(here_ref.shape[1]):
        wave_real = (spec_ref[0, mode, :window] * factor[...]).astype(bf16)
        wave_imag = (spec_ref[0, mode, window:] * factor[...]).astype(bf16)
        back_half = dot(jnp.concatenate([wave_real, wave_imag], axis=1), left_ref[...])
        back_wave = dot(right_ref[...], on_top(back_half.astype(bf16)))
        back_real, back_imag = back_wave[:window], back_wave[window:]
        probe_real, probe_imag = full_probe(here_ref, there_ref, meta_ref, mode)
        sums[0] = sums[0] + (probe_real * back_real + probe_imag * back_imag)
        sums[1] = sums[1] + (probe_real * back_imag - probe_imag * back_real)

    @pl.when(step == pl.num_programs(0) - 1)
    def _():
        row_start = scan_ref[slot]
        touched = pieces_ref.shape[2]
        deal = class_rows(touched, window, row_start, False)
        for part in range(2):
            dealt = dot(deal, sums[part].astype(bf16)).astype(bf16)
            for member in range(RUN):
                pieces_ref[member, part] = dealt[member * touched : (member + 1) * touched]


def place_kernel(
    meta_ref, scan_ref, above_ref, own_ref, partner_ref, upper_ref, lower_ref, half_ref
):
    chunks, _, chunk_rows, width = half_ref.shape
    height = chunks * chunk_rows
    _, touched, window = own_ref.shape
    quarters = chunks
    slots = 2 * quarters
    lane, quarter, member = meta_ref[0], meta_ref[1], meta_ref[5]
    mine, partners = lane * quarters + quarter, (1 - lane) * quarters + quarter
    first, second = quarter, quarters + quarter
    row_starts = (
        first_row(scan_ref[mine], member) - lane * height,
        first_row(scan_ref[partners], member) - lane * height,
        first_row(above_ref[first], member) - 2 * height,
        first_row(above_ref[second], member) - 2 * height,
    )
    col_starts = (
        scan_ref[slots + mine], scan_ref[slots + partners], above_ref[slots + first], above_ref[slots + second]
    )
    spread = jnp.concatenate([one_hot(window, width, start) for start in col_starts], axis=0)
    sources = (own_ref, partner_ref, upper_ref, lower_ref)
    shifts = [one_hot_down(height, touched, start) for start in row_starts]
    for part in range(2):
        moved = [dot(shift, source[part]).astype(bf16) for shift, source in zip(shifts, sources)]
        placed = dot(jnp.concatenate(moved, axis=1), spread).astype(bf16)
        for chunk in range(chunks):
            half_ref[chunk, part] = placed[chunk * chunk_rows : (chunk + 1) * chunk_rows]


def whole(shape):
    return pl.BlockSpec(shape, lambda step, *_: (0,) * len(shape))


def per_step(shape):
    return pl.BlockSpec((1,) + shape, lambda step, *_: (step,) + (0,) * len(shape))


def call(kernel, name, scalars, operands, in_specs, results, out_specs, steps=1, scratch=(), flops=0):
    return pl.pallas_call(
        kernel,
        grid_spec=pltpu.PrefetchScalarGridSpec(
            num_scalar_prefetch=len(scalars),
            grid=(steps,),
            in_specs=in_specs,
            out_specs=out_specs,
            scratch_shapes=scratch,
        ),
        out_shape=results,
        compiler_params=pltpu.CompilerParams(vmem_limit_bytes=VMEM_LIMIT),
        cost_estimate=pl.CostEstimate(
            flops=flops, bytes_accessed=4 * 1024 * 1024, transcendentals=0
        ),
        name=name,
    )(*scalars, *operands)


def on_device(
    object_field, probe_modes, measured_amplitude, row_offsets, col_offsets, position_counts
):
    window = probe_modes.shape[-1]
    slots = row_offsets.shape[1]
    width = object_field.shape[2]
    chunk_rows = object_field.shape[1]
    quarters = lax.axis_size("zq")
    tiles = lax.axis_size(TILE_AXES)
    lane, quarter, core = lax.axis_index("xl"), lax.axis_index("zq"), lax.axis_index("c")
    right, left = (jnp.asarray(table) for table in dft_blocks(window))
    swap = [(0, 1), (1, 0)]
    axes = TILE_AXES + ("xl",)
    up_first = [(2 * (t + 1), 2 * t) for t in range(tiles - 1)]
    up_second = [(2 * (t + 1), 2 * t + 1) for t in range(tiles - 1)]
    down_first = [(2 * t, 2 * (t + 1)) for t in range(tiles - 1)]
    down_second = [(2 * t + 1, 2 * (t + 1)) for t in range(tiles - 1)]
    downwards = [(t, t + 1) for t in range(tiles - 1)]

    up = lax.axis_index("y")
    member, tile = lax.axis_index("zr"), lax.axis_index(TILE_AXES)
    meta = jnp.stack([lane, quarter, core, tile, up * 2 + core, member, up]).astype(jnp.int32)
    scan = jnp.concatenate([row_offsets[0], col_offsets[0], position_counts])
    above = lax.ppermute(scan, TILE_AXES, downwards)

    ups = lax.axis_size("y")
    piece_rows = 2 * chunk_rows
    piece = lax.dynamic_slice_in_dim(probe_modes[0], (up * 2 + core) * piece_rows, piece_rows, axis=1)
    piece = jnp.concatenate([piece[:, :chunk_rows], piece[:, chunk_rows:]], axis=2)
    packed = jnp.concatenate([object_field, piece], axis=1).astype(bf16)
    packed = jnp.broadcast_to(packed[None], (quarters,) + packed.shape)
    packed = lax.all_to_all(packed, "zq", 0, 0, tiled=True)
    cut_shape = (2, quarters * chunk_rows, window)
    lane_shape = (quarters, 2, chunk_rows, width)
    own, partner, upper, lower, lane_modes = call(
        cut_kernel, "cut", (meta, scan, above), (packed,), [whole(packed.shape)],
        [jax.ShapeDtypeStruct(cut_shape, bf16)] * 4 + [jax.ShapeDtypeStruct(lane_shape, bf16)],
        [whole(cut_shape)] * 4 + [whole(lane_shape)],
    )
    other_modes = lax.ppermute(lane_modes, "xl", swap)
    other = lax.ppermute(partner, "xl", swap)
    below0 = lax.ppermute(upper, axes, up_first)
    below1 = lax.ppermute(lower, axes, up_second)
    lane_modes, other_modes, other, below0, below1 = lax.optimization_barrier(
        (lane_modes, other_modes, other, below0, below1)
    )
    part_modes = jnp.concatenate([lane_modes, other_modes], axis=0)
    shared = [
        lax.ppermute(part_modes, "y", [(i, (i + d) % ups) for i in range(ups)]) for d in range(1, ups)
    ]
    touched_shape = (2, window // RUN + CHUNK, window)
    touched = call(
        touch_kernel, "touch", (meta, scan), (own, other, below0, below1), [whole(cut_shape)] * 4,
        jax.ShapeDtypeStruct(touched_shape, bf16), whole(touched_shape),
    )
    touched = lax.all_gather(touched, "zr", axis=0)
    *shared, touched = lax.optimization_barrier((*shared, touched))
    here = jnp.stack([part_modes, *shared])
    there = lax.ppermute(here, "c", swap)
    window_shape = (2, window, window)

    modes = here.shape[1]
    at_once = modes // STEPS
    product_flops = modes * 2 * 2 * (2 * window) ** 2 * window
    probe_block = pl.BlockSpec(
        here.shape[:1] + (at_once,) + here.shape[2:], lambda step, *_: (0, step, 0, 0, 0)
    )
    spec_shape = (at_once, 2 * window, window)
    spectrum, power = call(
        forward_kernel, "forward", (meta, scan),
        (touched, here, there, right, left),
        [whole(touched.shape)] + [probe_block] * 2 + [whole(right.shape), whole(left.shape)],
        [
            jax.ShapeDtypeStruct((STEPS,) + spec_shape, f32),
            jax.ShapeDtypeStruct((window, window), bf16),
        ],
        [per_step(spec_shape), whole((window, window))],
        steps=STEPS,
        scratch=[pltpu.VMEM(window_shape, f32), pltpu.VMEM((window, window), f32)],
        flops=product_flops,
    )
    powers = lax.all_gather(power, "zr", axis=0)

    slot_block = pl.BlockSpec(
        (1, window, window), lambda step, meta_ref, *_: (meta_ref[0] * quarters + meta_ref[1], 0, 0)
    )
    pieces = call(
        backward_kernel, "backward", (meta, scan),
        (spectrum, powers, measured_amplitude[0], here, there, right, left),
        [per_step(spec_shape), whole(powers.shape), slot_block]
        + [probe_block] * 2 + [whole(right.shape), whole(left.shape)],
        jax.ShapeDtypeStruct(touched.shape, bf16),
        whole(touched.shape),
        steps=STEPS,
        scratch=[pltpu.VMEM((window, window), f32), pltpu.VMEM(window_shape, f32)],
        flops=product_flops,
    )
    pieces = lax.all_to_all(pieces, "zr", 0, 0, tiled=True)
    term = jnp.sum(pieces.astype(f32), axis=0).astype(bf16)
    partners = lax.ppermute(term, "xl", swap)
    above0 = lax.ppermute(term, axes, down_first)
    above1 = lax.ppermute(term, axes, down_second)
    half_sum = call(
        place_kernel, "place", (meta, scan, above), (term, partners, above0, above1),
        [whole(touched_shape)] * 4,
        jax.ShapeDtypeStruct(lane_shape, bf16), whole(lane_shape),
    )
    terms = lax.all_to_all(half_sum, "zq", 0, 0, tiled=True)
    return object_field - step_size * jnp.sum(terms.astype(f32), axis=0)


def solution(mesh):
    tiles, modes = mesh.devices.shape
    parts = Mesh(
        mesh.devices.reshape(tiles // 4, 2, 2, 2, 4, modes // 8), TILE_AXES + ("xl",) + DEPTH_AXES
    )
    tile, mode = TILE_AXES, ("xl",) + DEPTH_AXES
    placed = (
        P(None, tile + mode, None),
        P(mode, None, None, None),
        P(tile, None, None, None),
        P(tile, None),
        P(tile, None),
        P(),
    )
    return jax.shard_map(
        on_device,
        mesh=parts,
        in_specs=placed,
        out_specs=P(None, tile + mode, None),
        check_vma=False,
    )
```

```python
import math

import jax
import jax.numpy as jnp
import numpy as np
from jax import lax
from jax.experimental import pallas as pl
from jax.experimental.pallas import tpu as pltpu
from jax.sharding import Mesh, PartitionSpec as P

step_size = 0.05
f32 = jnp.float32
bf16 = jnp.bfloat16
TILE_AXES = ("y", "xh", "c")
DEPTH_AXES = ("zq", "zr")
CHUNK = 16
AT_ONCE = 2
QUARTERS = 4
RUN = 4
VMEM_LIMIT = 20 * 1024 * 1024


def dft_blocks(length):
    freqs = np.arange(length, dtype=np.int32)
    turns = freqs[:, None] * freqs[None, :] % length
    phase = turns.astype(np.float32) * np.float32(2.0 * math.pi / length)
    norm_scale = np.float32(1.0 / math.sqrt(length))
    cos_table = (np.cos(phase) * norm_scale).astype(jnp.bfloat16)
    sin_table = (-np.sin(phase) * norm_scale).astype(jnp.bfloat16)
    right = np.block([[cos_table, sin_table], [-sin_table, cos_table]])
    left = np.block([[cos_table, -sin_table], [sin_table, cos_table]])
    return right, left


def dot(left_side, right_side):
    return jnp.dot(left_side, right_side, preferred_element_type=f32)


def on_top(beside):
    size = beside.shape[1] // 2
    return jnp.concatenate([beside[:, :size], beside[:, size:]], axis=0)


def one_hot(rows, columns, offset):
    row = lax.broadcasted_iota(jnp.int32, (rows, columns), 0)
    column = lax.broadcasted_iota(jnp.int32, (rows, columns), 1)
    return (column == row + offset).astype(f32).astype(bf16)


def one_hot_down(rows, columns, offset):
    row = lax.broadcasted_iota(jnp.int32, (rows, columns), 0)
    column = lax.broadcasted_iota(jnp.int32, (rows, columns), 1)
    return (row == column + offset).astype(f32).astype(bf16)


def first_row(row_start, member):
    return (row_start // CHUNK - member + RUN - 1) // RUN * CHUNK


def class_rows(touched, window, row_start, across):
    blocks = []
    for member in range(RUN):
        spots, rows = ((1, touched), (window, 1)) if across else ((touched, 1), (1, window))
        spot = lax.broadcasted_iota(jnp.int32, spots, 1 if across else 0)
        row = lax.broadcasted_iota(jnp.int32, rows, 0 if across else 1)
        target = spot + spot // CHUNK * (CHUNK * (RUN - 1))
        first = first_row(row_start, member) * RUN + member * CHUNK - row_start
        blocks.append((target + first == row).astype(f32).astype(bf16))
    return jnp.concatenate(blocks, axis=1 if across else 0)


def cut_kernel(
    meta_ref, scan_ref, above_ref, packed_ref, own_ref, partner_ref, upper_ref, lower_ref, probe_ref
):
    chunks, _, _, width = packed_ref.shape
    window = own_ref.shape[-1]
    quarters = chunks
    slots = 2 * quarters
    lane, quarter = meta_ref[0], meta_ref[1]
    starts = (
        scan_ref[slots + lane * quarters + quarter],
        scan_ref[slots + (1 - lane) * quarters + quarter],
        above_ref[slots + quarter],
        above_ref[slots + quarters + quarter],
    )
    pick = jnp.concatenate([one_hot_down(width, window, start) for start in starts], axis=1)
    for part in range(2):
        rows = jnp.concatenate([packed_ref[chunk, part, :CHUNK] for chunk in range(chunks)], axis=0)
        columns = dot(rows, pick).astype(bf16)
        for index, target in enumerate((own_ref, partner_ref, upper_ref, lower_ref)):
            target[part] = columns[:, index * window : (index + 1) * window]
        for chunk in range(chunks):
            probe_ref[chunk, part] = packed_ref[chunk, part, CHUNK:]


def touch_kernel(
    meta_ref, scan_ref, own_ref, other_ref, below0_ref, below1_ref, touched_ref
):
    lane, quarter, member = meta_ref[0], meta_ref[1], meta_ref[5]
    height = own_ref.shape[1]
    touched = touched_ref.shape[1]
    row_start = scan_ref[lane * QUARTERS + quarter]
    first = first_row(row_start, member)
    pick = jnp.concatenate(
        [
            one_hot(touched, height, first - lane * height),
            one_hot(touched, height, first - (1 - lane) * height),
            one_hot(touched, height, first - 2 * height),
        ],
        axis=1,
    )
    for part in range(2):
        below = below0_ref[part] + below1_ref[part]
        stack = jnp.concatenate([own_ref[part], other_ref[part], below], axis=0)
        touched_ref[part] = dot(pick, stack).astype(bf16)


def full_probe(here_ref, there_ref, meta_ref, mode):
    core, up = meta_ref[2], meta_ref[6]
    count = here_ref.shape[0]
    window = here_ref.shape[-1] // 2

    def rows(part):
        pieces = []
        for row in range(count):
            place = lax.rem(up - row + count, count)
            here, there = here_ref[place, mode, part], there_ref[place, mode, part]
            for piece in (jnp.where(core == 0, here, there), jnp.where(core == 0, there, here)):
                pieces += [piece[:, :window], piece[:, window:]]
        return jnp.concatenate(pieces, axis=0).astype(f32)

    return rows(0), rows(1)


def forward_kernel(
    meta_ref, scan_ref, touched_ref, here_ref, there_ref, right_ref, left_ref,
    spec_ref, power_ref,
):
    lane, quarter = meta_ref[0], meta_ref[1]
    window = power_ref.shape[-1]
    row_start = scan_ref[lane * QUARTERS + quarter]
    pick = class_rows(touched_ref.shape[2], window, row_start, True)
    patch = [
        dot(pick, jnp.concatenate([touched_ref[member, part] for member in range(RUN)], axis=0))
        for part in range(2)
    ]
    total = jnp.zeros((window, window), f32)
    for start in range(0, spec_ref.shape[0], AT_ONCE):
        exits = []
        for mode in range(start, start + AT_ONCE):
            probe_real, probe_imag = full_probe(here_ref, there_ref, meta_ref, mode)
            exit_real = (probe_real * patch[0] - probe_imag * patch[1]).astype(bf16)
            exit_imag = (probe_real * patch[1] + probe_imag * patch[0]).astype(bf16)
            exits.append(jnp.concatenate([exit_real, exit_imag], axis=1))
        half_spectrum = dot(jnp.concatenate(exits, axis=0), right_ref[...]).astype(bf16)
        stacks = [on_top(half_spectrum[i * window : (i + 1) * window]) for i in range(AT_ONCE)]
        spectra = dot(left_ref[...], jnp.concatenate(stacks, axis=1))
        for i in range(AT_ONCE):
            spectrum = spectra[:, i * window : (i + 1) * window]
            spec_ref[start + i] = spectrum
            squares = spectrum * spectrum
            total = total + (squares[:window] + squares[window:])
    power_ref[...] = total.astype(bf16)


def backward_kernel(
    meta_ref, scan_ref, spec_ref, powers_ref, amplitude_ref, here_ref, there_ref, right_ref, left_ref,
    pieces_ref,
):
    slot = meta_ref[0] * QUARTERS + meta_ref[1]
    alive = slot < scan_ref[4 * QUARTERS + meta_ref[3]]
    window = pieces_ref.shape[-1]
    intensity = powers_ref[0].astype(f32)
    for member in range(1, powers_ref.shape[0]):
        intensity = intensity + powers_ref[member].astype(f32)
    correction = 1.0 - amplitude_ref[0, slot] / jnp.sqrt(intensity + 1.0)
    factor = jnp.where(alive, correction, 0.0)
    sums = [jnp.zeros((window, window), f32)] * 2
    for start in range(0, spec_ref.shape[0], AT_ONCE):
        waves = []
        for mode in range(start, start + AT_ONCE):
            wave_real = (spec_ref[mode, :window] * factor).astype(bf16)
            wave_imag = (spec_ref[mode, window:] * factor).astype(bf16)
            waves.append(jnp.concatenate([wave_real, wave_imag], axis=1))
        back_half = dot(jnp.concatenate(waves, axis=0), left_ref[...]).astype(bf16)
        stacks = [on_top(back_half[i * window : (i + 1) * window]) for i in range(AT_ONCE)]
        back_waves = dot(right_ref[...], jnp.concatenate(stacks, axis=1))
        for i in range(AT_ONCE):
            back_wave = back_waves[:, i * window : (i + 1) * window]
            back_real, back_imag = back_wave[:window], back_wave[window:]
            probe_real, probe_imag = full_probe(here_ref, there_ref, meta_ref, start + i)
            sums[0] = sums[0] + (probe_real * back_real + probe_imag * back_imag)
            sums[1] = sums[1] + (probe_real * back_imag - probe_imag * back_real)
    touched = pieces_ref.shape[2]
    deal = class_rows(touched, window, scan_ref[slot], False)
    for part in range(2):
        dealt = dot(deal, sums[part].astype(bf16)).astype(bf16)
        for member in range(RUN):
            pieces_ref[member, part] = dealt[member * touched : (member + 1) * touched]


def place_kernel(
    meta_ref, scan_ref, above_ref, own_ref, partner_ref, upper_ref, lower_ref, half_ref
):
    chunks, _, chunk_rows, width = half_ref.shape
    height = chunks * chunk_rows
    _, touched, window = own_ref.shape
    quarters = chunks
    slots = 2 * quarters
    lane, quarter, member = meta_ref[0], meta_ref[1], meta_ref[5]
    mine, partners = lane * quarters + quarter, (1 - lane) * quarters + quarter
    first, second = quarter, quarters + quarter
    row_starts = (
        first_row(scan_ref[mine], member) - lane * height,
        first_row(scan_ref[partners], member) - lane * height,
        first_row(above_ref[first], member) - 2 * height,
        first_row(above_ref[second], member) - 2 * height,
    )
    col_starts = (
        scan_ref[slots + mine], scan_ref[slots + partners], above_ref[slots + first], above_ref[slots + second]
    )
    spread = jnp.concatenate([one_hot(window, width, start) for start in col_starts], axis=0)
    sources = (own_ref, partner_ref, upper_ref, lower_ref)
    shifts = [one_hot_down(height, touched, start) for start in row_starts]
    for part in range(2):
        moved = [dot(shift, source[part]).astype(bf16) for shift, source in zip(shifts, sources)]
        placed = dot(jnp.concatenate(moved, axis=1), spread).astype(bf16)
        for chunk in range(chunks):
            half_ref[chunk, part] = placed[chunk * chunk_rows : (chunk + 1) * chunk_rows]


def call(kernel, name, scalars, operands, results, away=(), away_results=(), scratch=(), flops=0):
    held, far = pl.BlockSpec(memory_space=pltpu.VMEM), pl.BlockSpec(memory_space=pltpu.HBM)
    out_specs = held
    if isinstance(results, list):
        out_specs = [far if i in away_results else held for i in range(len(results))]
    return pl.pallas_call(
        kernel,
        grid_spec=pltpu.PrefetchScalarGridSpec(
            num_scalar_prefetch=len(scalars),
            grid=(1,),
            in_specs=[far if i in away else held for i in range(len(operands))],
            out_specs=out_specs,
            scratch_shapes=scratch,
        ),
        out_shape=results,
        compiler_params=pltpu.CompilerParams(vmem_limit_bytes=VMEM_LIMIT),
        cost_estimate=pl.CostEstimate(
            flops=flops, bytes_accessed=4 * 1024 * 1024, transcendentals=0
        ),
        name=name,
    )(*scalars, *operands)


def on_device(
    object_field, probe_modes, measured_amplitude, row_offsets, col_offsets, position_counts
):
    window = probe_modes.shape[-1]
    slots = row_offsets.shape[1]
    width = object_field.shape[2]
    chunk_rows = object_field.shape[1]
    quarters = lax.axis_size("zq")
    tiles = lax.axis_size(TILE_AXES)
    lane, quarter, core = lax.axis_index("xl"), lax.axis_index("zq"), lax.axis_index("c")
    right, left = (jnp.asarray(table) for table in dft_blocks(window))
    swap = [(0, 1), (1, 0)]
    axes = TILE_AXES + ("xl",)
    up_first = [(2 * (t + 1), 2 * t) for t in range(tiles - 1)]
    up_second = [(2 * (t + 1), 2 * t + 1) for t in range(tiles - 1)]
    down_first = [(2 * t, 2 * (t + 1)) for t in range(tiles - 1)]
    down_second = [(2 * t + 1, 2 * (t + 1)) for t in range(tiles - 1)]
    downwards = [(t, t + 1) for t in range(tiles - 1)]

    up = lax.axis_index("y")
    member, tile = lax.axis_index("zr"), lax.axis_index(TILE_AXES)
    meta = jnp.stack([lane, quarter, core, tile, up * 2 + core, member, up]).astype(jnp.int32)
    scan = jnp.concatenate([row_offsets[0], col_offsets[0], position_counts])
    above = lax.ppermute(scan, TILE_AXES, downwards)

    ups = lax.axis_size("y")
    piece_rows = 2 * chunk_rows
    piece = lax.dynamic_slice_in_dim(probe_modes[0], (up * 2 + core) * piece_rows, piece_rows, axis=1)
    piece = jnp.concatenate([piece[:, :chunk_rows], piece[:, chunk_rows:]], axis=2)
    packed = jnp.concatenate([object_field, piece], axis=1).astype(bf16)
    packed = jnp.broadcast_to(packed[None], (quarters,) + packed.shape)
    packed = lax.all_to_all(packed, "zq", 0, 0, tiled=True)
    cut_shape = (2, quarters * chunk_rows, window)
    lane_shape = (quarters, 2, chunk_rows, width)
    own, partner, upper, lower, lane_modes = call(
        cut_kernel, "cut", (meta, scan, above), (packed,),
        [jax.ShapeDtypeStruct(cut_shape, bf16)] * 4 + [jax.ShapeDtypeStruct(lane_shape, bf16)],
    )
    other_modes = lax.ppermute(lane_modes, "xl", swap)
    other = lax.ppermute(partner, "xl", swap)
    below0 = lax.ppermute(upper, axes, up_first)
    below1 = lax.ppermute(lower, axes, up_second)
    lane_modes, other_modes, other, below0, below1 = lax.optimization_barrier(
        (lane_modes, other_modes, other, below0, below1)
    )
    part_modes = jnp.concatenate([lane_modes, other_modes], axis=0)
    shared = [
        lax.ppermute(part_modes, "y", [(i, (i + d) % ups) for i in range(ups)]) for d in range(1, ups)
    ]
    touched_shape = (2, window // RUN + CHUNK, window)
    touched = call(
        touch_kernel, "touch", (meta, scan), (own, other, below0, below1),
        jax.ShapeDtypeStruct(touched_shape, bf16),
    )
    touched = lax.all_gather(touched, "zr", axis=0)
    *shared, touched = lax.optimization_barrier((*shared, touched))
    here = jnp.stack([part_modes, *shared])
    there = lax.ppermute(here, "c", swap)
    modes = here.shape[1]
    product_flops = modes * 2 * 2 * (2 * window) ** 2 * window
    spectrum, power = call(
        forward_kernel, "forward", (meta, scan), (touched, here, there, right, left),
        [
            jax.ShapeDtypeStruct((modes, 2 * window, window), f32),
            jax.ShapeDtypeStruct((window, window), bf16),
        ],
        flops=product_flops,
    )
    powers = lax.all_gather(power, "zr", axis=0)
    pieces = call(
        backward_kernel, "backward", (meta, scan),
        (spectrum, powers, measured_amplitude, here, there, right, left),
        jax.ShapeDtypeStruct(touched.shape, bf16),
        flops=product_flops,
    )
    pieces = lax.all_to_all(pieces, "zr", 0, 0, tiled=True)
    first, second, third, fourth = (pieces[sender].astype(f32) for sender in range(RUN))
    term = ((first + second) + (third + fourth)).astype(bf16)
    partners = lax.ppermute(term, "xl", swap)
    above0 = lax.ppermute(term, axes, down_first)
    above1 = lax.ppermute(term, axes, down_second)
    half_sum = call(
        place_kernel, "place", (meta, scan, above), (term, partners, above0, above1),
        jax.ShapeDtypeStruct(lane_shape, bf16),
    )
    terms = lax.all_to_all(half_sum, "zq", 0, 0, tiled=True)
    return object_field - step_size * jnp.sum(terms.astype(f32), axis=0)


def solution(mesh):
    tiles, modes = mesh.devices.shape
    parts = Mesh(
        mesh.devices.reshape(tiles // 4, 2, 2, 2, 4, modes // 8), TILE_AXES + ("xl",) + DEPTH_AXES
    )
    tile, mode = TILE_AXES, ("xl",) + DEPTH_AXES
    placed = (
        P(None, tile + mode, None),
        P(mode, None, None, None),
        P(tile, None, None, None),
        P(tile, None),
        P(tile, None),
        P(),
    )
    return jax.shard_map(
        on_device,
        mesh=parts,
        in_specs=placed,
        out_specs=P(None, tile + mode, None),
        check_vma=False,
    )
```

```python
import math

import jax
import jax.numpy as jnp
import numpy as np
from jax import lax
from jax.experimental import pallas as pl
from jax.experimental.pallas import tpu as pltpu
from jax.sharding import Mesh, PartitionSpec as P

step_size = 0.05
f32 = jnp.float32
bf16 = jnp.bfloat16
TILE_AXES = ("y", "xh", "c")
DEPTH_AXES = ("zq", "zr")
CHUNK = 16
AT_ONCE = 2
QUARTERS = 4
RUN = 4
VMEM_LIMIT = 20 * 1024 * 1024


def dft_blocks(length):
    freqs = np.arange(length, dtype=np.int32)
    turns = freqs[:, None] * freqs[None, :] % length
    phase = turns.astype(np.float32) * np.float32(2.0 * math.pi / length)
    norm_scale = np.float32(1.0 / math.sqrt(length))
    cos_table = (np.cos(phase) * norm_scale).astype(jnp.bfloat16)
    sin_table = (-np.sin(phase) * norm_scale).astype(jnp.bfloat16)
    right = np.block([[cos_table, sin_table], [-sin_table, cos_table]])
    left = np.block([[cos_table, -sin_table], [sin_table, cos_table]])
    return right, left


def dot(left_side, right_side):
    return jnp.dot(left_side, right_side, preferred_element_type=f32)


def on_top(beside):
    size = beside.shape[1] // 2
    return jnp.concatenate([beside[:, :size], beside[:, size:]], axis=0)


def one_hot(rows, columns, offset):
    row = lax.broadcasted_iota(jnp.int32, (rows, columns), 0)
    column = lax.broadcasted_iota(jnp.int32, (rows, columns), 1)
    return (column == row + offset).astype(f32).astype(bf16)


def one_hot_down(rows, columns, offset):
    row = lax.broadcasted_iota(jnp.int32, (rows, columns), 0)
    column = lax.broadcasted_iota(jnp.int32, (rows, columns), 1)
    return (row == column + offset).astype(f32).astype(bf16)


def first_row(row_start, member):
    return (row_start // CHUNK - member + RUN - 1) // RUN * CHUNK


def class_rows(touched, window, row_start, across):
    blocks = []
    for member in range(RUN):
        spots, rows = ((1, touched), (window, 1)) if across else ((touched, 1), (1, window))
        spot = lax.broadcasted_iota(jnp.int32, spots, 1 if across else 0)
        row = lax.broadcasted_iota(jnp.int32, rows, 0 if across else 1)
        target = spot + spot // CHUNK * (CHUNK * (RUN - 1))
        first = first_row(row_start, member) * RUN + member * CHUNK - row_start
        blocks.append((target + first == row).astype(f32).astype(bf16))
    return jnp.concatenate(blocks, axis=1 if across else 0)


def cut_kernel(
    meta_ref, scan_ref, above_ref, packed_ref, own_ref, upper_ref, lower_ref, swap_ref
):
    chunks, _, _, width = packed_ref.shape
    window = own_ref.shape[-1]
    quarters = chunks
    slots = 2 * quarters
    lane, quarter = meta_ref[0], meta_ref[1]
    starts = (
        scan_ref[slots + lane * quarters + quarter],
        scan_ref[slots + (1 - lane) * quarters + quarter],
        above_ref[slots + quarter],
        above_ref[slots + quarters + quarter],
    )
    pick = jnp.concatenate([one_hot_down(width, window, start) for start in starts], axis=1)
    for part in range(2):
        rows = jnp.concatenate([packed_ref[chunk, part, :CHUNK] for chunk in range(chunks)], axis=0)
        columns = dot(rows, pick).astype(bf16)
        for index, target in ((0, own_ref), (2, upper_ref), (3, lower_ref)):
            target[part] = columns[:, index * window : (index + 1) * window]
        for chunk in range(chunks):
            swap_ref[chunk, part] = packed_ref[chunk, part, CHUNK:]
        partner = columns[:, window : 2 * window]
        for pair in range(chunks // 2):
            swap_ref[chunks + pair, part] = jnp.concatenate(
                [partner[(2 * pair + i) * CHUNK : (2 * pair + i + 1) * CHUNK] for i in range(2)], axis=1
            )


def touch_kernel(
    meta_ref, scan_ref, own_ref, swapped_ref, below0_ref, below1_ref, touched_ref
):
    lane, quarter, member = meta_ref[0], meta_ref[1], meta_ref[5]
    height, window = own_ref.shape[1:]
    touched = touched_ref.shape[1]
    row_start = scan_ref[lane * QUARTERS + quarter]
    first = first_row(row_start, member)
    pick = jnp.concatenate(
        [
            one_hot(touched, height, first - lane * height),
            one_hot(touched, height, first - (1 - lane) * height),
            one_hot(touched, height, first - 2 * height),
        ],
        axis=1,
    )
    for part in range(2):
        below = below0_ref[part] + below1_ref[part]
        other = []
        for pair in range(QUARTERS, swapped_ref.shape[0]):
            beside = swapped_ref[pair, part]
            other += [beside[:, :window], beside[:, window:]]
        stack = jnp.concatenate([own_ref[part], *other, below], axis=0)
        touched_ref[part] = dot(pick, stack).astype(bf16)


def full_probe(here_ref, there_ref, meta_ref, mode):
    core, up = meta_ref[2], meta_ref[6]
    count = here_ref.shape[0]
    window = here_ref.shape[-1] // 2

    def rows(part):
        pieces = []
        for row in range(count):
            place = lax.rem(up - row + count, count)
            here, there = here_ref[place, mode, part], there_ref[place, mode, part]
            for piece in (jnp.where(core == 0, here, there), jnp.where(core == 0, there, here)):
                pieces += [piece[:, :window], piece[:, window:]]
        return jnp.concatenate(pieces, axis=0).astype(f32)

    return rows(0), rows(1)


def forward_kernel(
    meta_ref, scan_ref, touched_ref, here_ref, there_ref, right_ref, left_ref,
    spec_ref, power_ref,
):
    lane, quarter = meta_ref[0], meta_ref[1]
    window = power_ref.shape[-1]
    row_start = scan_ref[lane * QUARTERS + quarter]
    pick = class_rows(touched_ref.shape[2], window, row_start, True)
    patch = [
        dot(pick, jnp.concatenate([touched_ref[member, part] for member in range(RUN)], axis=0))
        for part in range(2)
    ]
    total = jnp.zeros((window, window), f32)
    for start in range(0, spec_ref.shape[0], AT_ONCE):
        exits = []
        for mode in range(start, start + AT_ONCE):
            probe_real, probe_imag = full_probe(here_ref, there_ref, meta_ref, mode)
            exit_real = (probe_real * patch[0] - probe_imag * patch[1]).astype(bf16)
            exit_imag = (probe_real * patch[1] + probe_imag * patch[0]).astype(bf16)
            exits.append(jnp.concatenate([exit_real, exit_imag], axis=1))
        half_spectrum = dot(jnp.concatenate(exits, axis=0), right_ref[...]).astype(bf16)
        stacks = [on_top(half_spectrum[i * window : (i + 1) * window]) for i in range(AT_ONCE)]
        spectra = dot(left_ref[...], jnp.concatenate(stacks, axis=1))
        for i in range(AT_ONCE):
            spectrum = spectra[:, i * window : (i + 1) * window]
            spec_ref[start + i] = spectrum
            squares = spectrum * spectrum
            total = total + (squares[:window] + squares[window:])
    power_ref[...] = total.astype(bf16)


def backward_kernel(
    meta_ref, scan_ref, spec_ref, powers_ref, amplitude_ref, here_ref, there_ref, right_ref, left_ref,
    pieces_ref,
):
    slot = meta_ref[0] * QUARTERS + meta_ref[1]
    alive = slot < scan_ref[4 * QUARTERS + meta_ref[3]]
    window = pieces_ref.shape[-1]
    intensity = powers_ref[0].astype(f32)
    for member in range(1, powers_ref.shape[0]):
        intensity = intensity + powers_ref[member].astype(f32)
    correction = 1.0 - amplitude_ref[0, slot] / jnp.sqrt(intensity + 1.0)
    factor = jnp.where(alive, correction, 0.0)
    sums = [jnp.zeros((window, window), f32)] * 2
    for start in range(0, spec_ref.shape[0], AT_ONCE):
        waves = []
        for mode in range(start, start + AT_ONCE):
            wave_real = (spec_ref[mode, :window] * factor).astype(bf16)
            wave_imag = (spec_ref[mode, window:] * factor).astype(bf16)
            waves.append(jnp.concatenate([wave_real, wave_imag], axis=1))
        back_half = dot(jnp.concatenate(waves, axis=0), left_ref[...]).astype(bf16)
        stacks = [on_top(back_half[i * window : (i + 1) * window]) for i in range(AT_ONCE)]
        back_waves = dot(right_ref[...], jnp.concatenate(stacks, axis=1))
        for i in range(AT_ONCE):
            back_wave = back_waves[:, i * window : (i + 1) * window]
            back_real, back_imag = back_wave[:window], back_wave[window:]
            probe_real, probe_imag = full_probe(here_ref, there_ref, meta_ref, start + i)
            sums[0] = sums[0] + (probe_real * back_real + probe_imag * back_imag)
            sums[1] = sums[1] + (probe_real * back_imag - probe_imag * back_real)
    touched = pieces_ref.shape[2]
    deal = class_rows(touched, window, scan_ref[slot], False)
    for part in range(2):
        dealt = dot(deal, sums[part].astype(bf16)).astype(bf16)
        for member in range(RUN):
            pieces_ref[member, part] = dealt[member * touched : (member + 1) * touched]


def place_kernel(
    meta_ref, scan_ref, above_ref, own_ref, partner_ref, upper_ref, lower_ref, half_ref
):
    chunks, _, chunk_rows, width = half_ref.shape
    height = chunks * chunk_rows
    _, touched, window = own_ref.shape
    quarters = chunks
    slots = 2 * quarters
    lane, quarter, member = meta_ref[0], meta_ref[1], meta_ref[5]
    mine, partners = lane * quarters + quarter, (1 - lane) * quarters + quarter
    first, second = quarter, quarters + quarter
    row_starts = (
        first_row(scan_ref[mine], member) - lane * height,
        first_row(scan_ref[partners], member) - lane * height,
        first_row(above_ref[first], member) - 2 * height,
        first_row(above_ref[second], member) - 2 * height,
    )
    col_starts = (
        scan_ref[slots + mine], scan_ref[slots + partners], above_ref[slots + first], above_ref[slots + second]
    )
    spread = jnp.concatenate([one_hot(window, width, start) for start in col_starts], axis=0)
    sources = (own_ref, partner_ref, upper_ref, lower_ref)
    shifts = [one_hot_down(height, touched, start) for start in row_starts]
    for part in range(2):
        moved = [dot(shift, source[part]).astype(bf16) for shift, source in zip(shifts, sources)]
        placed = dot(jnp.concatenate(moved, axis=1), spread).astype(bf16)
        for chunk in range(chunks):
            half_ref[chunk, part] = placed[chunk * chunk_rows : (chunk + 1) * chunk_rows]


def call(kernel, name, scalars, operands, results, away=(), away_results=(), scratch=(), flops=0):
    held, far = pl.BlockSpec(memory_space=pltpu.VMEM), pl.BlockSpec(memory_space=pltpu.HBM)
    out_specs = held
    if isinstance(results, list):
        out_specs = [far if i in away_results else held for i in range(len(results))]
    return pl.pallas_call(
        kernel,
        grid_spec=pltpu.PrefetchScalarGridSpec(
            num_scalar_prefetch=len(scalars),
            grid=(1,),
            in_specs=[far if i in away else held for i in range(len(operands))],
            out_specs=out_specs,
            scratch_shapes=scratch,
        ),
        out_shape=results,
        compiler_params=pltpu.CompilerParams(vmem_limit_bytes=VMEM_LIMIT),
        cost_estimate=pl.CostEstimate(
            flops=flops, bytes_accessed=4 * 1024 * 1024, transcendentals=0
        ),
        name=name,
    )(*scalars, *operands)


def on_device(
    object_field, probe_modes, measured_amplitude, row_offsets, col_offsets, position_counts
):
    window = probe_modes.shape[-1]
    slots = row_offsets.shape[1]
    width = object_field.shape[2]
    chunk_rows = object_field.shape[1]
    quarters = lax.axis_size("zq")
    tiles = lax.axis_size(TILE_AXES)
    lane, quarter, core = lax.axis_index("xl"), lax.axis_index("zq"), lax.axis_index("c")
    right, left = (jnp.asarray(table) for table in dft_blocks(window))
    swap = [(0, 1), (1, 0)]
    axes = TILE_AXES + ("xl",)
    up_first = [(2 * (t + 1), 2 * t) for t in range(tiles - 1)]
    up_second = [(2 * (t + 1), 2 * t + 1) for t in range(tiles - 1)]
    down_first = [(2 * t, 2 * (t + 1)) for t in range(tiles - 1)]
    down_second = [(2 * t + 1, 2 * (t + 1)) for t in range(tiles - 1)]
    downwards = [(t, t + 1) for t in range(tiles - 1)]

    up = lax.axis_index("y")
    member, tile = lax.axis_index("zr"), lax.axis_index(TILE_AXES)
    meta = jnp.stack([lane, quarter, core, tile, up * 2 + core, member, up]).astype(jnp.int32)
    scan = jnp.concatenate([row_offsets[0], col_offsets[0], position_counts])
    above = lax.ppermute(scan, TILE_AXES, downwards)

    ups = lax.axis_size("y")
    piece_rows = 2 * chunk_rows
    piece = lax.dynamic_slice_in_dim(probe_modes[0], (up * 2 + core) * piece_rows, piece_rows, axis=1)
    piece = jnp.concatenate([piece[:, :chunk_rows], piece[:, chunk_rows:]], axis=2)
    packed = jnp.concatenate([object_field, piece], axis=1).astype(bf16)
    packed = jnp.broadcast_to(packed[None], (quarters,) + packed.shape)
    packed = lax.all_to_all(packed, "zq", 0, 0, tiled=True)
    cut_shape = (2, quarters * chunk_rows, window)
    lane_shape = (quarters, 2, chunk_rows, width)
    own, upper, lower, to_swap = call(
        cut_kernel, "cut", (meta, scan, above), (packed,),
        [jax.ShapeDtypeStruct(cut_shape, bf16)] * 3
        + [jax.ShapeDtypeStruct((quarters + quarters // 2,) + lane_shape[1:], bf16)],
    )
    swapped = lax.ppermute(to_swap, "xl", swap)
    below0 = lax.ppermute(upper, axes, up_first)
    below1 = lax.ppermute(lower, axes, up_second)
    to_swap, swapped, below0, below1 = lax.optimization_barrier((to_swap, swapped, below0, below1))
    lane_modes, other_modes = to_swap[:quarters], swapped[:quarters]
    part_modes = jnp.concatenate([lane_modes, other_modes], axis=0)
    shared = [
        lax.ppermute(part_modes, "y", [(i, (i + d) % ups) for i in range(ups)]) for d in range(1, ups)
    ]
    touched_shape = (2, window // RUN + CHUNK, window)
    touched = call(
        touch_kernel, "touch", (meta, scan), (own, swapped, below0, below1),
        jax.ShapeDtypeStruct(touched_shape, bf16),
    )
    touched = lax.all_gather(touched, "zr", axis=0)
    *shared, touched = lax.optimization_barrier((*shared, touched))
    here = jnp.stack([part_modes, *shared])
    there = lax.ppermute(here, "c", swap)
    modes = here.shape[1]
    product_flops = modes * 2 * 2 * (2 * window) ** 2 * window
    spectrum, power = call(
        forward_kernel, "forward", (meta, scan), (touched, here, there, right, left),
        [
            jax.ShapeDtypeStruct((modes, 2 * window, window), f32),
            jax.ShapeDtypeStruct((window, window), bf16),
        ],
        flops=product_flops,
    )
    powers = lax.all_gather(power, "zr", axis=0)
    pieces = call(
        backward_kernel, "backward", (meta, scan),
        (spectrum, powers, measured_amplitude, here, there, right, left),
        jax.ShapeDtypeStruct(touched.shape, bf16),
        flops=product_flops,
    )
    pieces = lax.all_to_all(pieces, "zr", 0, 0, tiled=True)
    first, second, third, fourth = (pieces[sender].astype(f32) for sender in range(RUN))
    term = ((first + second) + (third + fourth)).astype(bf16)
    partners = lax.ppermute(term, "xl", swap)
    above0 = lax.ppermute(term, axes, down_first)
    above1 = lax.ppermute(term, axes, down_second)
    half_sum = call(
        place_kernel, "place", (meta, scan, above), (term, partners, above0, above1),
        jax.ShapeDtypeStruct(lane_shape, bf16),
    )
    terms = lax.all_to_all(half_sum, "zq", 0, 0, tiled=True)
    return object_field - step_size * jnp.sum(terms.astype(f32), axis=0)


def solution(mesh):
    tiles, modes = mesh.devices.shape
    parts = Mesh(
        mesh.devices.reshape(tiles // 4, 2, 2, 2, 4, modes // 8), TILE_AXES + ("xl",) + DEPTH_AXES
    )
    tile, mode = TILE_AXES, ("xl",) + DEPTH_AXES
    placed = (
        P(None, tile + mode, None),
        P(mode, None, None, None),
        P(tile, None, None, None),
        P(tile, None),
        P(tile, None),
        P(),
    )
    return jax.shard_map(
        on_device,
        mesh=parts,
        in_specs=placed,
        out_specs=P(None, tile + mode, None),
        check_vma=False,
    )
```

```python
import math

import jax
import jax.numpy as jnp
import numpy as np
from jax import lax
from jax.experimental import pallas as pl
from jax.experimental.pallas import tpu as pltpu
from jax.sharding import Mesh, PartitionSpec as P

step_size = 0.05
f32 = jnp.float32
bf16 = jnp.bfloat16
TILE_AXES = ("y", "xh", "c")
DEPTH_AXES = ("zq", "zr")
CHUNK = 16
AT_ONCE = 2
QUARTERS = 4
RUN = 4
VMEM_LIMIT = 20 * 1024 * 1024


def dft_blocks(length):
    freqs = np.arange(length, dtype=np.int32)
    turns = freqs[:, None] * freqs[None, :] % length
    phase = turns.astype(np.float32) * np.float32(2.0 * math.pi / length)
    norm_scale = np.float32(1.0 / math.sqrt(length))
    cos_table = (np.cos(phase) * norm_scale).astype(jnp.bfloat16)
    sin_table = (-np.sin(phase) * norm_scale).astype(jnp.bfloat16)
    right = np.block([[cos_table, sin_table], [-sin_table, cos_table]])
    left = np.block([[cos_table, -sin_table], [sin_table, cos_table]])
    return right, left


def dot(left_side, right_side):
    return jnp.dot(left_side, right_side, preferred_element_type=f32)


def on_top(beside):
    size = beside.shape[1] // 2
    return jnp.concatenate([beside[:, :size], beside[:, size:]], axis=0)


def one_hot(rows, columns, offset):
    row = lax.broadcasted_iota(jnp.int32, (rows, columns), 0)
    column = lax.broadcasted_iota(jnp.int32, (rows, columns), 1)
    return (column == row + offset).astype(f32).astype(bf16)


def one_hot_down(rows, columns, offset):
    row = lax.broadcasted_iota(jnp.int32, (rows, columns), 0)
    column = lax.broadcasted_iota(jnp.int32, (rows, columns), 1)
    return (row == column + offset).astype(f32).astype(bf16)


def first_row(row_start, member):
    return (row_start // CHUNK - member + RUN - 1) // RUN * CHUNK


def class_rows(touched, window, row_start, across):
    blocks = []
    for member in range(RUN):
        spots, rows = ((1, touched), (window, 1)) if across else ((touched, 1), (1, window))
        spot = lax.broadcasted_iota(jnp.int32, spots, 1 if across else 0)
        row = lax.broadcasted_iota(jnp.int32, rows, 0 if across else 1)
        target = spot + spot // CHUNK * (CHUNK * (RUN - 1))
        first = first_row(row_start, member) * RUN + member * CHUNK - row_start
        blocks.append((target + first == row).astype(f32).astype(bf16))
    return jnp.concatenate(blocks, axis=1 if across else 0)


def cut_kernel(
    meta_ref, scan_ref, above_ref, packed_ref, own_ref, upper_ref, lower_ref, swap_ref
):
    chunks, _, _, width = packed_ref.shape
    window = own_ref.shape[-1]
    quarters = chunks
    slots = 2 * quarters
    lane, quarter = meta_ref[0], meta_ref[1]
    starts = (
        scan_ref[slots + lane * quarters + quarter],
        scan_ref[slots + (1 - lane) * quarters + quarter],
        above_ref[slots + quarter],
        above_ref[slots + quarters + quarter],
    )
    pick = jnp.concatenate([one_hot_down(width, window, start) for start in starts], axis=1)
    for part in range(2):
        rows = jnp.concatenate([packed_ref[chunk, part, :CHUNK] for chunk in range(chunks)], axis=0)
        columns = dot(rows, pick).astype(bf16)
        for index, target in ((0, own_ref), (2, upper_ref), (3, lower_ref)):
            target[part] = columns[:, index * window : (index + 1) * window]
        for chunk in range(chunks):
            swap_ref[chunk, part] = packed_ref[chunk, part, CHUNK:]
        partner = columns[:, window : 2 * window]
        for pair in range(chunks // 2):
            swap_ref[chunks + pair, part] = jnp.concatenate(
                [partner[(2 * pair + i) * CHUNK : (2 * pair + i + 1) * CHUNK] for i in range(2)], axis=1
            )


def touch_kernel(
    meta_ref, scan_ref, own_ref, swapped_ref, below0_ref, below1_ref, touched_ref
):
    lane, quarter, member = meta_ref[0], meta_ref[1], meta_ref[5]
    height, window = own_ref.shape[1:]
    touched = touched_ref.shape[1]
    row_start = scan_ref[lane * QUARTERS + quarter]
    first = first_row(row_start, member)
    pick = jnp.concatenate(
        [
            one_hot(touched, height, first - lane * height),
            one_hot(touched, height, first - (1 - lane) * height),
            one_hot(touched, height, first - 2 * height),
        ],
        axis=1,
    )
    for part in range(2):
        below = below0_ref[part] + below1_ref[part]
        other = []
        for pair in range(QUARTERS, swapped_ref.shape[0]):
            beside = swapped_ref[pair, part]
            other += [beside[:, :window], beside[:, window:]]
        stack = jnp.concatenate([own_ref[part], *other, below], axis=0)
        touched_ref[part] = dot(pick, stack).astype(bf16)


def full_probe(here_ref, there_ref, meta_ref, mode):
    core, up = meta_ref[2], meta_ref[6]
    count = here_ref.shape[0]
    window = here_ref.shape[-1] // 2

    def rows(part):
        pieces = []
        for row in range(count):
            place = lax.rem(up - row + count, count)
            here, there = here_ref[place, mode, part], there_ref[place, mode, part]
            for piece in (jnp.where(core == 0, here, there), jnp.where(core == 0, there, here)):
                pieces += [piece[:, :window], piece[:, window:]]
        return jnp.concatenate(pieces, axis=0).astype(f32)

    return rows(0), rows(1)


def half_product(source_ref, patch, meta_ref, modes, right):
    up, count = meta_ref[6], source_ref.shape[0]
    window = source_ref.shape[-1] // 2
    exits = []
    for mode in modes:
        probe = []
        for part in range(2):
            pieces = []
            for row in range(count):
                piece = source_ref[lax.rem(up - row + count, count), mode, part]
                pieces += [piece[:, :window], piece[:, window:]]
            probe.append(jnp.concatenate(pieces, axis=0).astype(f32))
        exit_real = (probe[0] * patch[0] - probe[1] * patch[1]).astype(bf16)
        exit_imag = (probe[0] * patch[1] + probe[1] * patch[0]).astype(bf16)
        exits.append(jnp.concatenate([exit_real, exit_imag], axis=1))
    return dot(jnp.concatenate(exits, axis=0), right).astype(bf16)


def begin_kernel(meta_ref, scan_ref, touched_ref, here_ref, right_ref, half_ref, patch_ref):
    lane, quarter, core = meta_ref[0], meta_ref[1], meta_ref[2]
    window = touched_ref.shape[-1]
    run = window // (2 * here_ref.shape[0])
    row_start = scan_ref[lane * QUARTERS + quarter]
    pick = class_rows(touched_ref.shape[2], window, row_start, True)
    patch = []
    for part in range(2):
        stack = jnp.concatenate([touched_ref[member, part] for member in range(RUN)], axis=0)
        full = dot(pick, stack)
        even, odd = (
            jnp.concatenate([full[i : i + run] for i in range(first, window, 2 * run)], axis=0)
            for first in (0, run)
        )
        patch.append(jnp.where(core == 0, even, odd))
        patch_ref[part] = jnp.where(core == 0, odd, even)
    rows = half_ref.shape[1]
    for start in range(0, half_ref.shape[0], AT_ONCE):
        modes = range(start, start + AT_ONCE)
        half = half_product(here_ref, patch, meta_ref, modes, right_ref[...])
        for i in range(AT_ONCE):
            half_ref[start + i] = half[i * rows : (i + 1) * rows]


def forward_kernel(
    meta_ref, half_ref, patch_ref, there_ref, right_ref, left_ref, spec_ref, power_ref
):
    core = meta_ref[2]
    window = power_ref.shape[-1]
    rows = half_ref.shape[1]
    run = window // (2 * there_ref.shape[0])
    patch = [patch_ref[part] for part in range(2)]
    total = jnp.zeros((window, window), f32)
    for start in range(0, spec_ref.shape[0], AT_ONCE):
        modes = range(start, start + AT_ONCE)
        others = half_product(there_ref, patch, meta_ref, modes, right_ref[...])
        stacks = []
        for i in range(AT_ONCE):
            here, there = half_ref[start + i], others[i * rows : (i + 1) * rows]
            even, odd = jnp.where(core == 0, here, there), jnp.where(core == 0, there, here)
            pieces = []
            for first in range(0, rows, run):
                pieces += [even[first : first + run], odd[first : first + run]]
            stacks.append(on_top(jnp.concatenate(pieces, axis=0)))
        spectra = dot(left_ref[...], jnp.concatenate(stacks, axis=1))
        for i in range(AT_ONCE):
            spectrum = spectra[:, i * window : (i + 1) * window]
            spec_ref[start + i] = spectrum
            squares = spectrum * spectrum
            total = total + (squares[:window] + squares[window:])
    power_ref[...] = total.astype(bf16)


def backward_kernel(
    meta_ref, scan_ref, spec_ref, powers_ref, amplitude_ref, here_ref, there_ref, right_ref, left_ref,
    pieces_ref,
):
    slot = meta_ref[0] * QUARTERS + meta_ref[1]
    alive = slot < scan_ref[4 * QUARTERS + meta_ref[3]]
    window = pieces_ref.shape[-1]
    intensity = powers_ref[0].astype(f32)
    for member in range(1, powers_ref.shape[0]):
        intensity = intensity + powers_ref[member].astype(f32)
    correction = 1.0 - amplitude_ref[0, slot] / jnp.sqrt(intensity + 1.0)
    factor = jnp.where(alive, correction, 0.0)
    sums = [jnp.zeros((window, window), f32)] * 2
    for start in range(0, spec_ref.shape[0], AT_ONCE):
        waves = []
        for mode in range(start, start + AT_ONCE):
            wave_real = (spec_ref[mode, :window] * factor).astype(bf16)
            wave_imag = (spec_ref[mode, window:] * factor).astype(bf16)
            waves.append(jnp.concatenate([wave_real, wave_imag], axis=1))
        back_half = dot(jnp.concatenate(waves, axis=0), left_ref[...]).astype(bf16)
        stacks = [on_top(back_half[i * window : (i + 1) * window]) for i in range(AT_ONCE)]
        back_waves = dot(right_ref[...], jnp.concatenate(stacks, axis=1))
        for i in range(AT_ONCE):
            back_wave = back_waves[:, i * window : (i + 1) * window]
            back_real, back_imag = back_wave[:window], back_wave[window:]
            probe_real, probe_imag = full_probe(here_ref, there_ref, meta_ref, start + i)
            sums[0] = sums[0] + (probe_real * back_real + probe_imag * back_imag)
            sums[1] = sums[1] + (probe_real * back_imag - probe_imag * back_real)
    touched = pieces_ref.shape[2]
    deal = class_rows(touched, window, scan_ref[slot], False)
    for part in range(2):
        dealt = dot(deal, sums[part].astype(bf16)).astype(bf16)
        for member in range(RUN):
            pieces_ref[member, part] = dealt[member * touched : (member + 1) * touched]


def place_kernel(
    meta_ref, scan_ref, above_ref, own_ref, partner_ref, upper_ref, lower_ref, half_ref
):
    chunks, _, chunk_rows, width = half_ref.shape
    height = chunks * chunk_rows
    _, touched, window = own_ref.shape
    quarters = chunks
    slots = 2 * quarters
    lane, quarter, member = meta_ref[0], meta_ref[1], meta_ref[5]
    mine, partners = lane * quarters + quarter, (1 - lane) * quarters + quarter
    first, second = quarter, quarters + quarter
    row_starts = (
        first_row(scan_ref[mine], member) - lane * height,
        first_row(scan_ref[partners], member) - lane * height,
        first_row(above_ref[first], member) - 2 * height,
        first_row(above_ref[second], member) - 2 * height,
    )
    col_starts = (
        scan_ref[slots + mine], scan_ref[slots + partners], above_ref[slots + first], above_ref[slots + second]
    )
    spread = jnp.concatenate([one_hot(window, width, start) for start in col_starts], axis=0)
    sources = (own_ref, partner_ref, upper_ref, lower_ref)
    shifts = [one_hot_down(height, touched, start) for start in row_starts]
    for part in range(2):
        moved = [dot(shift, source[part]).astype(bf16) for shift, source in zip(shifts, sources)]
        placed = dot(jnp.concatenate(moved, axis=1), spread).astype(bf16)
        for chunk in range(chunks):
            half_ref[chunk, part] = placed[chunk * chunk_rows : (chunk + 1) * chunk_rows]


def call(kernel, name, scalars, operands, results, away=(), away_results=(), scratch=(), flops=0):
    held, far = pl.BlockSpec(memory_space=pltpu.VMEM), pl.BlockSpec(memory_space=pltpu.HBM)
    out_specs = held
    if isinstance(results, list):
        out_specs = [far if i in away_results else held for i in range(len(results))]
    return pl.pallas_call(
        kernel,
        grid_spec=pltpu.PrefetchScalarGridSpec(
            num_scalar_prefetch=len(scalars),
            grid=(1,),
            in_specs=[far if i in away else held for i in range(len(operands))],
            out_specs=out_specs,
            scratch_shapes=scratch,
        ),
        out_shape=results,
        compiler_params=pltpu.CompilerParams(vmem_limit_bytes=VMEM_LIMIT),
        cost_estimate=pl.CostEstimate(
            flops=flops, bytes_accessed=4 * 1024 * 1024, transcendentals=0
        ),
        name=name,
    )(*scalars, *operands)


def on_device(
    object_field, probe_modes, measured_amplitude, row_offsets, col_offsets, position_counts
):
    window = probe_modes.shape[-1]
    slots = row_offsets.shape[1]
    width = object_field.shape[2]
    chunk_rows = object_field.shape[1]
    quarters = lax.axis_size("zq")
    tiles = lax.axis_size(TILE_AXES)
    lane, quarter, core = lax.axis_index("xl"), lax.axis_index("zq"), lax.axis_index("c")
    right, left = (jnp.asarray(table) for table in dft_blocks(window))
    swap = [(0, 1), (1, 0)]
    axes = TILE_AXES + ("xl",)
    up_first = [(2 * (t + 1), 2 * t) for t in range(tiles - 1)]
    up_second = [(2 * (t + 1), 2 * t + 1) for t in range(tiles - 1)]
    down_first = [(2 * t, 2 * (t + 1)) for t in range(tiles - 1)]
    down_second = [(2 * t + 1, 2 * (t + 1)) for t in range(tiles - 1)]
    downwards = [(t, t + 1) for t in range(tiles - 1)]

    up = lax.axis_index("y")
    member, tile = lax.axis_index("zr"), lax.axis_index(TILE_AXES)
    meta = jnp.stack([lane, quarter, core, tile, up * 2 + core, member, up]).astype(jnp.int32)
    scan = jnp.concatenate([row_offsets[0], col_offsets[0], position_counts])
    above = lax.ppermute(scan, TILE_AXES, downwards)

    ups = lax.axis_size("y")
    piece_rows = 2 * chunk_rows
    piece = lax.dynamic_slice_in_dim(probe_modes[0], (up * 2 + core) * piece_rows, piece_rows, axis=1)
    piece = jnp.concatenate([piece[:, :chunk_rows], piece[:, chunk_rows:]], axis=2)
    packed = jnp.concatenate([object_field, piece], axis=1).astype(bf16)
    packed = jnp.broadcast_to(packed[None], (quarters,) + packed.shape)
    packed = lax.all_to_all(packed, "zq", 0, 0, tiled=True)
    cut_shape = (2, quarters * chunk_rows, window)
    lane_shape = (quarters, 2, chunk_rows, width)
    own, upper, lower, to_swap = call(
        cut_kernel, "cut", (meta, scan, above), (packed,),
        [jax.ShapeDtypeStruct(cut_shape, bf16)] * 3
        + [jax.ShapeDtypeStruct((quarters + quarters // 2,) + lane_shape[1:], bf16)],
    )
    swapped = lax.ppermute(to_swap, "xl", swap)
    below0 = lax.ppermute(upper, axes, up_first)
    below1 = lax.ppermute(lower, axes, up_second)
    to_swap, swapped, below0, below1 = lax.optimization_barrier((to_swap, swapped, below0, below1))
    lane_modes, other_modes = to_swap[:quarters], swapped[:quarters]
    part_modes = jnp.concatenate([lane_modes, other_modes], axis=0)
    shared = [
        lax.ppermute(part_modes, "y", [(i, (i + d) % ups) for i in range(ups)]) for d in range(1, ups)
    ]
    touched_shape = (2, window // RUN + CHUNK, window)
    touched = call(
        touch_kernel, "touch", (meta, scan), (own, swapped, below0, below1),
        jax.ShapeDtypeStruct(touched_shape, bf16),
    )
    touched = lax.all_gather(touched, "zr", axis=0)
    *shared, touched = lax.optimization_barrier((*shared, touched))
    here = jnp.stack([part_modes, *shared])
    there = lax.ppermute(here, "c", swap)
    modes = here.shape[1]
    product_flops = modes * 2 * 2 * (2 * window) ** 2 * window
    half_spectra, other_patch = call(
        begin_kernel, "begin", (meta, scan), (touched, here, right),
        [
            jax.ShapeDtypeStruct((modes, window // 2, 2 * window), bf16),
            jax.ShapeDtypeStruct((2, window // 2, window), f32),
        ],
        flops=product_flops // 4,
    )
    spectrum, power = call(
        forward_kernel, "forward", (meta,), (half_spectra, other_patch, there, right, left),
        [
            jax.ShapeDtypeStruct((modes, 2 * window, window), f32),
            jax.ShapeDtypeStruct((window, window), bf16),
        ],
        flops=product_flops * 3 // 4,
    )
    powers = lax.all_gather(power, "zr", axis=0)
    pieces = call(
        backward_kernel, "backward", (meta, scan),
        (spectrum, powers, measured_amplitude, here, there, right, left),
        jax.ShapeDtypeStruct(touched.shape, bf16),
        flops=product_flops,
    )
    pieces = lax.all_to_all(pieces, "zr", 0, 0, tiled=True)
    first, second, third, fourth = (pieces[sender].astype(f32) for sender in range(RUN))
    term = ((first + second) + (third + fourth)).astype(bf16)
    partners = lax.ppermute(term, "xl", swap)
    above0 = lax.ppermute(term, axes, down_first)
    above1 = lax.ppermute(term, axes, down_second)
    half_sum = call(
        place_kernel, "place", (meta, scan, above), (term, partners, above0, above1),
        jax.ShapeDtypeStruct(lane_shape, bf16),
    )
    terms = lax.all_to_all(half_sum, "zq", 0, 0, tiled=True)
    return object_field - step_size * jnp.sum(terms.astype(f32), axis=0)


def solution(mesh):
    tiles, modes = mesh.devices.shape
    parts = Mesh(
        mesh.devices.reshape(tiles // 4, 2, 2, 2, 4, modes // 8), TILE_AXES + ("xl",) + DEPTH_AXES
    )
    tile, mode = TILE_AXES, ("xl",) + DEPTH_AXES
    placed = (
        P(None, tile + mode, None),
        P(mode, None, None, None),
        P(tile, None, None, None),
        P(tile, None),
        P(tile, None),
        P(),
    )
    return jax.shard_map(
        on_device,
        mesh=parts,
        in_specs=placed,
        out_specs=P(None, tile + mode, None),
        check_vma=False,
    )
```

```python
import math

import jax
import jax.numpy as jnp
import numpy as np
from jax import lax
from jax.experimental import pallas as pl
from jax.experimental.pallas import tpu as pltpu
from jax.sharding import Mesh, PartitionSpec as P

step_size = 0.05
f32 = jnp.float32
bf16 = jnp.bfloat16
TILE_AXES = ("y", "xh", "c")
DEPTH_AXES = ("zq", "zr")
CHUNK = 16
AT_ONCE = 2
QUARTERS = 4
RUN = 4
VMEM_LIMIT = 20 * 1024 * 1024


def dft_blocks(length):
    freqs = np.arange(length, dtype=np.int32)
    turns = freqs[:, None] * freqs[None, :] % length
    phase = turns.astype(np.float32) * np.float32(2.0 * math.pi / length)
    norm_scale = np.float32(1.0 / math.sqrt(length))
    cos_table = (np.cos(phase) * norm_scale).astype(jnp.bfloat16)
    sin_table = (-np.sin(phase) * norm_scale).astype(jnp.bfloat16)
    right = np.block([[cos_table, sin_table], [-sin_table, cos_table]])
    left = np.block([[cos_table, -sin_table], [sin_table, cos_table]])
    return right, left


def dot(left_side, right_side):
    return jnp.dot(left_side, right_side, preferred_element_type=f32)


def on_top(beside):
    size = beside.shape[1] // 2
    return jnp.concatenate([beside[:, :size], beside[:, size:]], axis=0)


def one_hot(rows, columns, offset):
    row = lax.broadcasted_iota(jnp.int32, (rows, columns), 0)
    column = lax.broadcasted_iota(jnp.int32, (rows, columns), 1)
    return (column == row + offset).astype(f32).astype(bf16)


def one_hot_down(rows, columns, offset):
    row = lax.broadcasted_iota(jnp.int32, (rows, columns), 0)
    column = lax.broadcasted_iota(jnp.int32, (rows, columns), 1)
    return (row == column + offset).astype(f32).astype(bf16)


def first_row(row_start, member):
    return (row_start // CHUNK - member + RUN - 1) // RUN * CHUNK


def class_rows(touched, window, row_start, across):
    blocks = []
    for member in range(RUN):
        spots, rows = ((1, touched), (window, 1)) if across else ((touched, 1), (1, window))
        spot = lax.broadcasted_iota(jnp.int32, spots, 1 if across else 0)
        row = lax.broadcasted_iota(jnp.int32, rows, 0 if across else 1)
        target = spot + spot // CHUNK * (CHUNK * (RUN - 1))
        first = first_row(row_start, member) * RUN + member * CHUNK - row_start
        blocks.append((target + first == row).astype(f32).astype(bf16))
    return jnp.concatenate(blocks, axis=1 if across else 0)


def cut_kernel(
    meta_ref, scan_ref, above_ref, packed_ref, own_ref, upper_ref, lower_ref, swap_ref
):
    chunks, _, _, width = packed_ref.shape
    window = own_ref.shape[-1]
    quarters = chunks
    slots = 2 * quarters
    lane, quarter = meta_ref[0], meta_ref[1]
    starts = (
        scan_ref[slots + lane * quarters + quarter],
        scan_ref[slots + (1 - lane) * quarters + quarter],
        above_ref[slots + quarter],
        above_ref[slots + quarters + quarter],
    )
    pick = jnp.concatenate([one_hot_down(width, window, start) for start in starts], axis=1)
    for part in range(2):
        rows = jnp.concatenate([packed_ref[chunk, part, :CHUNK] for chunk in range(chunks)], axis=0)
        columns = dot(rows, pick).astype(bf16)
        for index, target in ((0, own_ref), (2, upper_ref), (3, lower_ref)):
            target[part] = columns[:, index * window : (index + 1) * window]
        for chunk in range(chunks):
            swap_ref[chunk, part] = packed_ref[chunk, part, CHUNK:]
        partner = columns[:, window : 2 * window]
        for pair in range(chunks // 2):
            swap_ref[chunks + pair, part] = jnp.concatenate(
                [partner[(2 * pair + i) * CHUNK : (2 * pair + i + 1) * CHUNK] for i in range(2)], axis=1
            )


def touch_kernel(
    meta_ref, scan_ref, own_ref, swapped_ref, below0_ref, below1_ref, touched_ref
):
    lane, quarter, member = meta_ref[0], meta_ref[1], meta_ref[5]
    height, window = own_ref.shape[1:]
    touched = touched_ref.shape[1]
    row_start = scan_ref[lane * QUARTERS + quarter]
    first = first_row(row_start, member)
    pick = jnp.concatenate(
        [
            one_hot(touched, height, first - lane * height),
            one_hot(touched, height, first - (1 - lane) * height),
            one_hot(touched, height, first - 2 * height),
        ],
        axis=1,
    )
    for part in range(2):
        below = below0_ref[part] + below1_ref[part]
        other = []
        for pair in range(QUARTERS, swapped_ref.shape[0]):
            beside = swapped_ref[pair, part]
            other += [beside[:, :window], beside[:, window:]]
        stack = jnp.concatenate([own_ref[part], *other, below], axis=0)
        touched_ref[part] = dot(pick, stack).astype(bf16)


def full_probe(here_ref, there_ref, meta_ref, mode):
    core, up = meta_ref[2], meta_ref[6]
    count = here_ref.shape[0]
    window = here_ref.shape[-1] // 2

    def rows(part):
        pieces = []
        for row in range(count):
            place = lax.rem(up - row + count, count)
            here, there = here_ref[place, mode, part], there_ref[place, mode, part]
            for piece in (jnp.where(core == 0, here, there), jnp.where(core == 0, there, here)):
                pieces += [piece[:, :window], piece[:, window:]]
        return jnp.concatenate(pieces, axis=0).astype(f32)

    return rows(0), rows(1)


def half_product(source_ref, patch, meta_ref, modes, right):
    up, count = meta_ref[6], source_ref.shape[0]
    window = source_ref.shape[-1] // 2
    exits = []
    for mode in modes:
        probe = []
        for part in range(2):
            pieces = []
            for row in range(count):
                piece = source_ref[lax.rem(up - row + count, count), mode, part]
                pieces += [piece[:, :window], piece[:, window:]]
            probe.append(jnp.concatenate(pieces, axis=0).astype(f32))
        exit_real = (probe[0] * patch[0] - probe[1] * patch[1]).astype(bf16)
        exit_imag = (probe[0] * patch[1] + probe[1] * patch[0]).astype(bf16)
        exits.append(jnp.concatenate([exit_real, exit_imag], axis=1))
    return dot(jnp.concatenate(exits, axis=0), right).astype(bf16)


def begin_kernel(meta_ref, scan_ref, touched_ref, here_ref, right_ref, half_ref, patch_ref):
    lane, quarter, core = meta_ref[0], meta_ref[1], meta_ref[2]
    window = touched_ref.shape[-1]
    run = window // (2 * here_ref.shape[0])
    row_start = scan_ref[lane * QUARTERS + quarter]
    pick = class_rows(touched_ref.shape[2], window, row_start, True)
    patch = []
    for part in range(2):
        stack = jnp.concatenate([touched_ref[member, part] for member in range(RUN)], axis=0)
        full = dot(pick, stack)
        even, odd = (
            jnp.concatenate([full[i : i + run] for i in range(first, window, 2 * run)], axis=0)
            for first in (0, run)
        )
        patch.append(jnp.where(core == 0, even, odd))
        patch_ref[part] = jnp.where(core == 0, odd, even)
    rows = half_ref.shape[1]
    for start in range(0, half_ref.shape[0], AT_ONCE):
        modes = range(start, start + AT_ONCE)
        half = half_product(here_ref, patch, meta_ref, modes, right_ref[...])
        for i in range(AT_ONCE):
            half_ref[start + i] = half[i * rows : (i + 1) * rows]


def forward_kernel(
    meta_ref, half_ref, patch_ref, there_ref, right_ref, left_ref, spec_ref, power_ref
):
    core = meta_ref[2]
    window = power_ref.shape[-1]
    rows = half_ref.shape[1]
    run = window // (2 * there_ref.shape[0])
    patch = [patch_ref[part] for part in range(2)]
    total = jnp.zeros((window, window), f32)
    for start in range(0, spec_ref.shape[0], AT_ONCE):
        modes = range(start, start + AT_ONCE)
        others = half_product(there_ref, patch, meta_ref, modes, right_ref[...])
        stacks = []
        for i in range(AT_ONCE):
            here, there = half_ref[start + i], others[i * rows : (i + 1) * rows]
            even, odd = jnp.where(core == 0, here, there), jnp.where(core == 0, there, here)
            pieces = []
            for first in range(0, rows, run):
                pieces += [even[first : first + run], odd[first : first + run]]
            stacks.append(on_top(jnp.concatenate(pieces, axis=0)))
        spectra = dot(left_ref[...], jnp.concatenate(stacks, axis=1))
        for i in range(AT_ONCE):
            spectrum = spectra[:, i * window : (i + 1) * window]
            spec_ref[start + i] = spectrum
            squares = spectrum * spectrum
            total = total + (squares[:window] + squares[window:])
    power_ref[...] = total.astype(bf16)


def backward_kernel(
    meta_ref, scan_ref, spec_ref, powers_ref, amplitude_ref, here_ref, there_ref, right_ref, left_ref,
    pieces_ref,
):
    slot = meta_ref[0] * QUARTERS + meta_ref[1]
    alive = slot < scan_ref[4 * QUARTERS + meta_ref[3]]
    window = pieces_ref.shape[-1]
    intensity = powers_ref[0].astype(f32)
    for member in range(1, powers_ref.shape[0]):
        intensity = intensity + powers_ref[member].astype(f32)
    correction = 1.0 - amplitude_ref[0, slot] / jnp.sqrt(intensity + 1.0)
    factor = jnp.where(alive, correction, 0.0)
    sums = [jnp.zeros((window, window), f32)] * 2
    for start in range(0, spec_ref.shape[0], AT_ONCE):
        waves = []
        for mode in range(start, start + AT_ONCE):
            wave_real = (spec_ref[mode, :window] * factor).astype(bf16)
            wave_imag = (spec_ref[mode, window:] * factor).astype(bf16)
            waves.append(jnp.concatenate([wave_real, wave_imag], axis=1))
        back_half = dot(jnp.concatenate(waves, axis=0), left_ref[...]).astype(bf16)
        stacks = [on_top(back_half[i * window : (i + 1) * window]) for i in range(AT_ONCE)]
        back_waves = dot(right_ref[...], jnp.concatenate(stacks, axis=1))
        for i in range(AT_ONCE):
            back_wave = back_waves[:, i * window : (i + 1) * window]
            back_real, back_imag = back_wave[:window], back_wave[window:]
            probe_real, probe_imag = full_probe(here_ref, there_ref, meta_ref, start + i)
            sums[0] = sums[0] + (probe_real * back_real + probe_imag * back_imag)
            sums[1] = sums[1] + (probe_real * back_imag - probe_imag * back_real)
    touched = pieces_ref.shape[2]
    deal = class_rows(touched, window, scan_ref[slot], False)
    for part in range(2):
        dealt = dot(deal, sums[part].astype(bf16)).astype(bf16)
        for member in range(RUN):
            pieces_ref[member, part] = dealt[member * touched : (member + 1) * touched]


def place_kernel(
    meta_ref, scan_ref, above_ref, own_ref, partner_ref, upper_ref, lower_ref, half_ref
):
    chunks, _, chunk_rows, width = half_ref.shape
    height = chunks * chunk_rows
    _, touched, window = own_ref.shape
    quarters = chunks
    slots = 2 * quarters
    lane, quarter, member = meta_ref[0], meta_ref[1], meta_ref[5]
    mine, partners = lane * quarters + quarter, (1 - lane) * quarters + quarter
    first, second = quarter, quarters + quarter
    row_starts = (
        first_row(scan_ref[mine], member) - lane * height,
        first_row(scan_ref[partners], member) - lane * height,
        first_row(above_ref[first], member) - 2 * height,
        first_row(above_ref[second], member) - 2 * height,
    )
    col_starts = (
        scan_ref[slots + mine], scan_ref[slots + partners], above_ref[slots + first], above_ref[slots + second]
    )
    spread = jnp.concatenate([one_hot(window, width, start) for start in col_starts], axis=0)
    sources = (own_ref, partner_ref, upper_ref, lower_ref)
    shifts = [one_hot_down(height, touched, start) for start in row_starts]
    for part in range(2):
        moved = [dot(shift, source[part]).astype(bf16) for shift, source in zip(shifts, sources)]
        placed = dot(jnp.concatenate(moved, axis=1), spread).astype(bf16)
        for chunk in range(chunks):
            half_ref[chunk, part] = placed[chunk * chunk_rows : (chunk + 1) * chunk_rows]


def call(kernel, name, scalars, operands, results, away=(), away_results=(), scratch=(), flops=0):
    held, far = pl.BlockSpec(memory_space=pltpu.VMEM), pl.BlockSpec(memory_space=pltpu.HBM)
    out_specs = held
    if isinstance(results, list):
        out_specs = [far if i in away_results else held for i in range(len(results))]
    return pl.pallas_call(
        kernel,
        grid_spec=pltpu.PrefetchScalarGridSpec(
            num_scalar_prefetch=len(scalars),
            grid=(1,),
            in_specs=[far if i in away else held for i in range(len(operands))],
            out_specs=out_specs,
            scratch_shapes=scratch,
        ),
        out_shape=results,
        compiler_params=pltpu.CompilerParams(vmem_limit_bytes=VMEM_LIMIT),
        cost_estimate=pl.CostEstimate(
            flops=flops, bytes_accessed=4 * 1024 * 1024, transcendentals=0
        ),
        name=name,
    )(*scalars, *operands)


def on_device(
    object_field, probe_modes, measured_amplitude, row_offsets, col_offsets, position_counts
):
    window = probe_modes.shape[-1]
    slots = row_offsets.shape[1]
    width = object_field.shape[2]
    chunk_rows = object_field.shape[1]
    quarters = lax.axis_size("zq")
    tiles = lax.axis_size(TILE_AXES)
    lane, quarter, core = lax.axis_index("xl"), lax.axis_index("zq"), lax.axis_index("c")
    right, left = (jnp.asarray(table) for table in dft_blocks(window))
    swap = [(0, 1), (1, 0)]
    axes = TILE_AXES + ("xl",)
    up_first = [(2 * (t + 1), 2 * t) for t in range(tiles - 1)]
    up_second = [(2 * (t + 1), 2 * t + 1) for t in range(tiles - 1)]
    down_first = [(2 * t, 2 * (t + 1)) for t in range(tiles - 1)]
    down_second = [(2 * t + 1, 2 * (t + 1)) for t in range(tiles - 1)]
    downwards = [(t, t + 1) for t in range(tiles - 1)]

    up = lax.axis_index("y")
    member, tile = lax.axis_index("zr"), lax.axis_index(TILE_AXES)
    meta = jnp.stack([lane, quarter, core, tile, up * 2 + core, member, up]).astype(jnp.int32)
    scan = jnp.concatenate([row_offsets[0], col_offsets[0], position_counts])
    above = lax.ppermute(scan, TILE_AXES, downwards)

    ups = lax.axis_size("y")
    piece_rows = 2 * chunk_rows
    piece = lax.dynamic_slice_in_dim(probe_modes[0], (up * 2 + core) * piece_rows, piece_rows, axis=1)
    piece = jnp.concatenate([piece[:, :chunk_rows], piece[:, chunk_rows:]], axis=2)
    packed = jnp.concatenate([object_field, piece], axis=1).astype(bf16)
    packed = jnp.broadcast_to(packed[None], (quarters,) + packed.shape)
    packed = lax.all_to_all(packed, "zq", 0, 0, tiled=True)
    cut_shape = (2, quarters * chunk_rows, window)
    lane_shape = (quarters, 2, chunk_rows, width)
    own, upper, lower, to_swap = call(
        cut_kernel, "cut", (meta, scan, above), (packed,),
        [jax.ShapeDtypeStruct(cut_shape, bf16)] * 3
        + [jax.ShapeDtypeStruct((quarters + quarters // 2,) + lane_shape[1:], bf16)],
    )
    swapped = lax.ppermute(to_swap, "xl", swap)
    below0 = lax.ppermute(upper, axes, up_first)
    below1 = lax.ppermute(lower, axes, up_second)
    lane_modes, other_modes = to_swap[:quarters], swapped[:quarters]
    part_modes = jnp.concatenate([lane_modes, other_modes], axis=0)
    shared = [
        lax.ppermute(part_modes, "y", [(i, (i + d) % ups) for i in range(ups)]) for d in range(1, ups)
    ]
    touched_shape = (2, window // RUN + CHUNK, window)
    touched = call(
        touch_kernel, "touch", (meta, scan), (own, swapped, below0, below1),
        jax.ShapeDtypeStruct(touched_shape, bf16),
        flops=5 * 10**9,
    )
    touched = lax.all_gather(touched, "zr", axis=0)
    *shared, touched = lax.optimization_barrier((*shared, touched))
    here = jnp.stack([part_modes, *shared])
    there = lax.ppermute(here, "c", swap)
    modes = here.shape[1]
    product_flops = modes * 2 * 2 * (2 * window) ** 2 * window
    half_spectra, other_patch = call(
        begin_kernel, "begin", (meta, scan), (touched, here, right),
        [
            jax.ShapeDtypeStruct((modes, window // 2, 2 * window), bf16),
            jax.ShapeDtypeStruct((2, window // 2, window), f32),
        ],
        flops=product_flops // 4,
    )
    spectrum, power = call(
        forward_kernel, "forward", (meta,), (half_spectra, other_patch, there, right, left),
        [
            jax.ShapeDtypeStruct((modes, 2 * window, window), f32),
            jax.ShapeDtypeStruct((window, window), bf16),
        ],
        flops=product_flops * 3 // 4,
    )
    powers = lax.all_gather(power, "zr", axis=0)
    pieces = call(
        backward_kernel, "backward", (meta, scan),
        (spectrum, powers, measured_amplitude, here, there, right, left),
        jax.ShapeDtypeStruct(touched.shape, bf16),
        flops=product_flops,
    )
    pieces = lax.all_to_all(pieces, "zr", 0, 0, tiled=True)
    first, second, third, fourth = (pieces[sender].astype(f32) for sender in range(RUN))
    term = ((first + second) + (third + fourth)).astype(bf16)
    partners = lax.ppermute(term, "xl", swap)
    above0 = lax.ppermute(term, axes, down_first)
    above1 = lax.ppermute(term, axes, down_second)
    half_sum = call(
        place_kernel, "place", (meta, scan, above), (term, partners, above0, above1),
        jax.ShapeDtypeStruct(lane_shape, bf16),
    )
    terms = lax.all_to_all(half_sum, "zq", 0, 0, tiled=True)
    return object_field - step_size * jnp.sum(terms.astype(f32), axis=0)


def solution(mesh):
    tiles, modes = mesh.devices.shape
    parts = Mesh(
        mesh.devices.reshape(tiles // 4, 2, 2, 2, 4, modes // 8), TILE_AXES + ("xl",) + DEPTH_AXES
    )
    tile, mode = TILE_AXES, ("xl",) + DEPTH_AXES
    placed = (
        P(None, tile + mode, None),
        P(mode, None, None, None),
        P(tile, None, None, None),
        P(tile, None),
        P(tile, None),
        P(),
    )
    return jax.shard_map(
        on_device,
        mesh=parts,
        in_specs=placed,
        out_specs=P(None, tile + mode, None),
        check_vma=False,
    )
```

```python
import math

import jax
import jax.numpy as jnp
import numpy as np
from jax import lax
from jax.experimental import pallas as pl
from jax.experimental.pallas import tpu as pltpu
from jax.sharding import Mesh, PartitionSpec as P

step_size = 0.05
f32 = jnp.float32
bf16 = jnp.bfloat16
TILE_AXES = ("y", "xh", "c")
DEPTH_AXES = ("zq", "zr")
CHUNK = 16
AT_ONCE = 4
QUARTERS = 4
RUN = 4
VMEM_LIMIT = 20 * 1024 * 1024


def dft_blocks(length):
    freqs = np.arange(length, dtype=np.int32)
    turns = freqs[:, None] * freqs[None, :] % length
    phase = turns.astype(np.float32) * np.float32(2.0 * math.pi / length)
    norm_scale = np.float32(1.0 / math.sqrt(length))
    cos_table = (np.cos(phase) * norm_scale).astype(jnp.bfloat16)
    sin_table = (-np.sin(phase) * norm_scale).astype(jnp.bfloat16)
    right = np.block([[cos_table, sin_table], [-sin_table, cos_table]])
    left = np.block([[cos_table, -sin_table], [sin_table, cos_table]])
    return right, left


def dot(left_side, right_side):
    return jnp.dot(left_side, right_side, preferred_element_type=f32)


def on_top(beside):
    size = beside.shape[1] // 2
    return jnp.concatenate([beside[:, :size], beside[:, size:]], axis=0)


def one_hot(rows, columns, offset):
    row = lax.broadcasted_iota(jnp.int32, (rows, columns), 0)
    column = lax.broadcasted_iota(jnp.int32, (rows, columns), 1)
    return (column == row + offset).astype(f32).astype(bf16)


def one_hot_down(rows, columns, offset):
    row = lax.broadcasted_iota(jnp.int32, (rows, columns), 0)
    column = lax.broadcasted_iota(jnp.int32, (rows, columns), 1)
    return (row == column + offset).astype(f32).astype(bf16)


def first_row(row_start, member):
    return (row_start // CHUNK - member + RUN - 1) // RUN * CHUNK


def class_rows(touched, window, row_start, across):
    blocks = []
    for member in range(RUN):
        spots, rows = ((1, touched), (window, 1)) if across else ((touched, 1), (1, window))
        spot = lax.broadcasted_iota(jnp.int32, spots, 1 if across else 0)
        row = lax.broadcasted_iota(jnp.int32, rows, 0 if across else 1)
        target = spot + spot // CHUNK * (CHUNK * (RUN - 1))
        first = first_row(row_start, member) * RUN + member * CHUNK - row_start
        blocks.append((target + first == row).astype(f32).astype(bf16))
    return jnp.concatenate(blocks, axis=1 if across else 0)


def cut_kernel(
    meta_ref, scan_ref, above_ref, packed_ref, own_ref, upper_ref, lower_ref, swap_ref
):
    chunks, _, _, width = packed_ref.shape
    window = own_ref.shape[-1]
    quarters = chunks
    slots = 2 * quarters
    lane, quarter = meta_ref[0], meta_ref[1]
    starts = (
        scan_ref[slots + lane * quarters + quarter],
        scan_ref[slots + (1 - lane) * quarters + quarter],
        above_ref[slots + quarter],
        above_ref[slots + quarters + quarter],
    )
    pick = jnp.concatenate([one_hot_down(width, window, start) for start in starts], axis=1)
    for part in range(2):
        rows = jnp.concatenate([packed_ref[chunk, part, :CHUNK] for chunk in range(chunks)], axis=0)
        columns = dot(rows, pick).astype(bf16)
        for index, target in ((0, own_ref), (2, upper_ref), (3, lower_ref)):
            target[part] = columns[:, index * window : (index + 1) * window]
        for chunk in range(chunks):
            swap_ref[chunk, part] = packed_ref[chunk, part, CHUNK:]
        partner = columns[:, window : 2 * window]
        for pair in range(chunks // 2):
            swap_ref[chunks + pair, part] = jnp.concatenate(
                [partner[(2 * pair + i) * CHUNK : (2 * pair + i + 1) * CHUNK] for i in range(2)], axis=1
            )


def touch_kernel(
    meta_ref, scan_ref, own_ref, swapped_ref, below0_ref, below1_ref, touched_ref
):
    lane, quarter, member = meta_ref[0], meta_ref[1], meta_ref[5]
    height, window = own_ref.shape[1:]
    touched = touched_ref.shape[1]
    row_start = scan_ref[lane * QUARTERS + quarter]
    first = first_row(row_start, member)
    pick = jnp.concatenate(
        [
            one_hot(touched, height, first - lane * height),
            one_hot(touched, height, first - (1 - lane) * height),
            one_hot(touched, height, first - 2 * height),
        ],
        axis=1,
    )
    for part in range(2):
        below = below0_ref[part] + below1_ref[part]
        other = []
        for pair in range(QUARTERS, swapped_ref.shape[0]):
            beside = swapped_ref[pair, part]
            other += [beside[:, :window], beside[:, window:]]
        stack = jnp.concatenate([own_ref[part], *other, below], axis=0)
        touched_ref[part] = dot(pick, stack).astype(bf16)


def full_probe(here_ref, there_ref, meta_ref, mode):
    core, up = meta_ref[2], meta_ref[6]
    count = here_ref.shape[0]
    window = here_ref.shape[-1] // 2

    def rows(part):
        pieces = []
        for row in range(count):
            place = lax.rem(up - row + count, count)
            here, there = here_ref[place, mode, part], there_ref[place, mode, part]
            for piece in (jnp.where(core == 0, here, there), jnp.where(core == 0, there, here)):
                pieces += [piece[:, :window], piece[:, window:]]
        return jnp.concatenate(pieces, axis=0).astype(f32)

    return rows(0), rows(1)


def half_product(source_ref, patch, meta_ref, modes, right):
    up, count = meta_ref[6], source_ref.shape[0]
    window = source_ref.shape[-1] // 2
    exits = []
    for mode in modes:
        probe = []
        for part in range(2):
            pieces = []
            for row in range(count):
                piece = source_ref[lax.rem(up - row + count, count), mode, part]
                pieces += [piece[:, :window], piece[:, window:]]
            probe.append(jnp.concatenate(pieces, axis=0).astype(f32))
        exit_real = (probe[0] * patch[0] - probe[1] * patch[1]).astype(bf16)
        exit_imag = (probe[0] * patch[1] + probe[1] * patch[0]).astype(bf16)
        exits.append(jnp.concatenate([exit_real, exit_imag], axis=1))
    return dot(jnp.concatenate(exits, axis=0), right).astype(bf16)


def begin_kernel(meta_ref, scan_ref, touched_ref, here_ref, right_ref, half_ref, patch_ref):
    lane, quarter, core = meta_ref[0], meta_ref[1], meta_ref[2]
    window = touched_ref.shape[-1]
    run = window // (2 * here_ref.shape[0])
    row_start = scan_ref[lane * QUARTERS + quarter]
    pick = class_rows(touched_ref.shape[2], window, row_start, True)
    patch = []
    for part in range(2):
        stack = jnp.concatenate([touched_ref[member, part] for member in range(RUN)], axis=0)
        full = dot(pick, stack)
        even, odd = (
            jnp.concatenate([full[i : i + run] for i in range(first, window, 2 * run)], axis=0)
            for first in (0, run)
        )
        patch.append(jnp.where(core == 0, even, odd))
        patch_ref[part] = jnp.where(core == 0, odd, even)
    rows = half_ref.shape[1]
    for start in range(0, half_ref.shape[0], AT_ONCE):
        modes = range(start, start + AT_ONCE)
        half = half_product(here_ref, patch, meta_ref, modes, right_ref[...])
        for i in range(AT_ONCE):
            half_ref[start + i] = half[i * rows : (i + 1) * rows]


def forward_kernel(
    meta_ref, half_ref, patch_ref, there_ref, right_ref, left_ref, spec_ref, power_ref
):
    core = meta_ref[2]
    window = power_ref.shape[-1]
    rows = half_ref.shape[1]
    run = window // (2 * there_ref.shape[0])
    patch = [patch_ref[part] for part in range(2)]
    total = jnp.zeros((window, window), f32)
    for start in range(0, spec_ref.shape[0], AT_ONCE):
        modes = range(start, start + AT_ONCE)
        others = half_product(there_ref, patch, meta_ref, modes, right_ref[...])
        stacks = []
        for i in range(AT_ONCE):
            here, there = half_ref[start + i], others[i * rows : (i + 1) * rows]
            even, odd = jnp.where(core == 0, here, there), jnp.where(core == 0, there, here)
            pieces = []
            for first in range(0, rows, run):
                pieces += [even[first : first + run], odd[first : first + run]]
            stacks.append(on_top(jnp.concatenate(pieces, axis=0)))
        spectra = dot(left_ref[...], jnp.concatenate(stacks, axis=1))
        for i in range(AT_ONCE):
            spectrum = spectra[:, i * window : (i + 1) * window]
            spec_ref[start + i] = spectrum
            squares = spectrum * spectrum
            total = total + (squares[:window] + squares[window:])
    power_ref[...] = total.astype(bf16)


def backward_kernel(
    meta_ref, scan_ref, spec_ref, powers_ref, amplitude_ref, here_ref, there_ref, right_ref, left_ref,
    pieces_ref,
):
    slot = meta_ref[0] * QUARTERS + meta_ref[1]
    alive = slot < scan_ref[4 * QUARTERS + meta_ref[3]]
    window = pieces_ref.shape[-1]
    intensity = powers_ref[0].astype(f32)
    for member in range(1, powers_ref.shape[0]):
        intensity = intensity + powers_ref[member].astype(f32)
    correction = 1.0 - amplitude_ref[0, slot] / jnp.sqrt(intensity + 1.0)
    factor = jnp.where(alive, correction, 0.0)
    sums = [jnp.zeros((window, window), f32)] * 2
    for start in range(0, spec_ref.shape[0], AT_ONCE):
        waves = []
        for mode in range(start, start + AT_ONCE):
            wave_real = (spec_ref[mode, :window] * factor).astype(bf16)
            wave_imag = (spec_ref[mode, window:] * factor).astype(bf16)
            waves.append(jnp.concatenate([wave_real, wave_imag], axis=1))
        back_half = dot(jnp.concatenate(waves, axis=0), left_ref[...]).astype(bf16)
        stacks = [on_top(back_half[i * window : (i + 1) * window]) for i in range(AT_ONCE)]
        back_waves = dot(right_ref[...], jnp.concatenate(stacks, axis=1))
        for i in range(AT_ONCE):
            back_wave = back_waves[:, i * window : (i + 1) * window]
            back_real, back_imag = back_wave[:window], back_wave[window:]
            probe_real, probe_imag = full_probe(here_ref, there_ref, meta_ref, start + i)
            sums[0] = sums[0] + (probe_real * back_real + probe_imag * back_imag)
            sums[1] = sums[1] + (probe_real * back_imag - probe_imag * back_real)
    touched = pieces_ref.shape[2]
    deal = class_rows(touched, window, scan_ref[slot], False)
    for part in range(2):
        dealt = dot(deal, sums[part].astype(bf16)).astype(bf16)
        for member in range(RUN):
            pieces_ref[member, part] = dealt[member * touched : (member + 1) * touched]


def place_kernel(
    meta_ref, scan_ref, above_ref, own_ref, partner_ref, upper_ref, lower_ref, half_ref
):
    chunks, _, chunk_rows, width = half_ref.shape
    height = chunks * chunk_rows
    _, touched, window = own_ref.shape
    quarters = chunks
    slots = 2 * quarters
    lane, quarter, member = meta_ref[0], meta_ref[1], meta_ref[5]
    mine, partners = lane * quarters + quarter, (1 - lane) * quarters + quarter
    first, second = quarter, quarters + quarter
    row_starts = (
        first_row(scan_ref[mine], member) - lane * height,
        first_row(scan_ref[partners], member) - lane * height,
        first_row(above_ref[first], member) - 2 * height,
        first_row(above_ref[second], member) - 2 * height,
    )
    col_starts = (
        scan_ref[slots + mine], scan_ref[slots + partners], above_ref[slots + first], above_ref[slots + second]
    )
    spread = jnp.concatenate([one_hot(window, width, start) for start in col_starts], axis=0)
    sources = (own_ref, partner_ref, upper_ref, lower_ref)
    shifts = [one_hot_down(height, touched, start) for start in row_starts]
    for part in range(2):
        moved = [dot(shift, source[part]).astype(bf16) for shift, source in zip(shifts, sources)]
        placed = dot(jnp.concatenate(moved, axis=1), spread).astype(bf16)
        for chunk in range(chunks):
            half_ref[chunk, part] = placed[chunk * chunk_rows : (chunk + 1) * chunk_rows]


def call(kernel, name, scalars, operands, results, away=(), away_results=(), scratch=(), flops=0):
    held, far = pl.BlockSpec(memory_space=pltpu.VMEM), pl.BlockSpec(memory_space=pltpu.HBM)
    out_specs = held
    if isinstance(results, list):
        out_specs = [far if i in away_results else held for i in range(len(results))]
    return pl.pallas_call(
        kernel,
        grid_spec=pltpu.PrefetchScalarGridSpec(
            num_scalar_prefetch=len(scalars),
            grid=(1,),
            in_specs=[far if i in away else held for i in range(len(operands))],
            out_specs=out_specs,
            scratch_shapes=scratch,
        ),
        out_shape=results,
        compiler_params=pltpu.CompilerParams(vmem_limit_bytes=VMEM_LIMIT),
        cost_estimate=pl.CostEstimate(
            flops=flops, bytes_accessed=4 * 1024 * 1024, transcendentals=0
        ),
        name=name,
    )(*scalars, *operands)


def on_device(
    object_field, probe_modes, measured_amplitude, row_offsets, col_offsets, position_counts
):
    window = probe_modes.shape[-1]
    slots = row_offsets.shape[1]
    width = object_field.shape[2]
    chunk_rows = object_field.shape[1]
    quarters = lax.axis_size("zq")
    tiles = lax.axis_size(TILE_AXES)
    lane, quarter, core = lax.axis_index("xl"), lax.axis_index("zq"), lax.axis_index("c")
    right, left = (jnp.asarray(table) for table in dft_blocks(window))
    swap = [(0, 1), (1, 0)]
    axes = TILE_AXES + ("xl",)
    up_first = [(2 * (t + 1), 2 * t) for t in range(tiles - 1)]
    up_second = [(2 * (t + 1), 2 * t + 1) for t in range(tiles - 1)]
    down_first = [(2 * t, 2 * (t + 1)) for t in range(tiles - 1)]
    down_second = [(2 * t + 1, 2 * (t + 1)) for t in range(tiles - 1)]
    downwards = [(t, t + 1) for t in range(tiles - 1)]

    up = lax.axis_index("y")
    member, tile = lax.axis_index("zr"), lax.axis_index(TILE_AXES)
    meta = jnp.stack([lane, quarter, core, tile, up * 2 + core, member, up]).astype(jnp.int32)
    scan = jnp.concatenate([row_offsets[0], col_offsets[0], position_counts])
    above = lax.ppermute(scan, TILE_AXES, downwards)

    ups = lax.axis_size("y")
    piece_rows = 2 * chunk_rows
    piece = lax.dynamic_slice_in_dim(probe_modes[0], (up * 2 + core) * piece_rows, piece_rows, axis=1)
    piece = jnp.concatenate([piece[:, :chunk_rows], piece[:, chunk_rows:]], axis=2)
    packed = jnp.concatenate([object_field, piece], axis=1).astype(bf16)
    packed = jnp.broadcast_to(packed[None], (quarters,) + packed.shape)
    packed = lax.all_to_all(packed, "zq", 0, 0, tiled=True)
    cut_shape = (2, quarters * chunk_rows, window)
    lane_shape = (quarters, 2, chunk_rows, width)
    own, upper, lower, to_swap = call(
        cut_kernel, "cut", (meta, scan, above), (packed,),
        [jax.ShapeDtypeStruct(cut_shape, bf16)] * 3
        + [jax.ShapeDtypeStruct((quarters + quarters // 2,) + lane_shape[1:], bf16)],
    )
    swapped = lax.ppermute(to_swap, "xl", swap)
    below0 = lax.ppermute(upper, axes, up_first)
    below1 = lax.ppermute(lower, axes, up_second)
    to_swap, swapped, below0, below1 = lax.optimization_barrier((to_swap, swapped, below0, below1))
    lane_modes, other_modes = to_swap[:quarters], swapped[:quarters]
    part_modes = jnp.concatenate([lane_modes, other_modes], axis=0)
    shared = [
        lax.ppermute(part_modes, "y", [(i, (i + d) % ups) for i in range(ups)]) for d in range(1, ups)
    ]
    touched_shape = (2, window // RUN + CHUNK, window)
    touched = call(
        touch_kernel, "touch", (meta, scan), (own, swapped, below0, below1),
        jax.ShapeDtypeStruct(touched_shape, bf16),
    )
    touched = lax.all_gather(touched, "zr", axis=0)
    *shared, touched = lax.optimization_barrier((*shared, touched))
    here = jnp.stack([part_modes, *shared])
    there = lax.ppermute(here, "c", swap)
    modes = here.shape[1]
    product_flops = modes * 2 * 2 * (2 * window) ** 2 * window
    half_spectra, other_patch = call(
        begin_kernel, "begin", (meta, scan), (touched, here, right),
        [
            jax.ShapeDtypeStruct((modes, window // 2, 2 * window), bf16),
            jax.ShapeDtypeStruct((2, window // 2, window), f32),
        ],
        flops=product_flops // 4,
    )
    spectrum, power = call(
        forward_kernel, "forward", (meta,), (half_spectra, other_patch, there, right, left),
        [
            jax.ShapeDtypeStruct((modes, 2 * window, window), f32),
            jax.ShapeDtypeStruct((window, window), bf16),
        ],
        flops=product_flops * 3 // 4,
    )
    powers = lax.all_gather(power, "zr", axis=0)
    pieces = call(
        backward_kernel, "backward", (meta, scan),
        (spectrum, powers, measured_amplitude, here, there, right, left),
        jax.ShapeDtypeStruct(touched.shape, bf16),
        flops=product_flops,
    )
    pieces = lax.all_to_all(pieces, "zr", 0, 0, tiled=True)
    first, second, third, fourth = (pieces[sender].astype(f32) for sender in range(RUN))
    term = ((first + second) + (third + fourth)).astype(bf16)
    partners = lax.ppermute(term, "xl", swap)
    above0 = lax.ppermute(term, axes, down_first)
    above1 = lax.ppermute(term, axes, down_second)
    half_sum = call(
        place_kernel, "place", (meta, scan, above), (term, partners, above0, above1),
        jax.ShapeDtypeStruct(lane_shape, bf16),
    )
    terms = lax.all_to_all(half_sum, "zq", 0, 0, tiled=True)
    return object_field - step_size * jnp.sum(terms.astype(f32), axis=0)


def solution(mesh):
    tiles, modes = mesh.devices.shape
    parts = Mesh(
        mesh.devices.reshape(tiles // 4, 2, 2, 2, 4, modes // 8), TILE_AXES + ("xl",) + DEPTH_AXES
    )
    tile, mode = TILE_AXES, ("xl",) + DEPTH_AXES
    placed = (
        P(None, tile + mode, None),
        P(mode, None, None, None),
        P(tile, None, None, None),
        P(tile, None),
        P(tile, None),
        P(),
    )
    return jax.shard_map(
        on_device,
        mesh=parts,
        in_specs=placed,
        out_specs=P(None, tile + mode, None),
        check_vma=False,
    )
```

```python
import math

import jax
import jax.numpy as jnp
import numpy as np
from jax import lax
from jax.experimental import pallas as pl
from jax.experimental.pallas import tpu as pltpu
from jax.sharding import Mesh, PartitionSpec as P

step_size = 0.05
f32 = jnp.float32
bf16 = jnp.bfloat16
TILE_AXES = ("y", "xh", "c")
DEPTH_AXES = ("zq", "zr")
CHUNK = 16
AT_ONCE = 4
QUARTERS = 4
RUN = 4
VMEM_LIMIT = 20 * 1024 * 1024


def dft_blocks(length):
    freqs = np.arange(length, dtype=np.int32)
    turns = freqs[:, None] * freqs[None, :] % length
    phase = turns.astype(np.float32) * np.float32(2.0 * math.pi / length)
    norm_scale = np.float32(1.0 / math.sqrt(length))
    cos_table = (np.cos(phase) * norm_scale).astype(jnp.bfloat16)
    sin_table = (-np.sin(phase) * norm_scale).astype(jnp.bfloat16)
    right = np.block([[cos_table, sin_table], [-sin_table, cos_table]])
    left = np.block([[cos_table, -sin_table], [sin_table, cos_table]])
    return right, left


def dot(left_side, right_side):
    return jnp.dot(left_side, right_side, preferred_element_type=f32)


def on_top(beside):
    size = beside.shape[1] // 2
    return jnp.concatenate([beside[:, :size], beside[:, size:]], axis=0)


def one_hot(rows, columns, offset):
    row = lax.broadcasted_iota(jnp.int32, (rows, columns), 0)
    column = lax.broadcasted_iota(jnp.int32, (rows, columns), 1)
    return (column == row + offset).astype(f32).astype(bf16)


def one_hot_down(rows, columns, offset):
    row = lax.broadcasted_iota(jnp.int32, (rows, columns), 0)
    column = lax.broadcasted_iota(jnp.int32, (rows, columns), 1)
    return (row == column + offset).astype(f32).astype(bf16)


def first_row(row_start, member):
    return (row_start // CHUNK - member + RUN - 1) // RUN * CHUNK


def class_rows(touched, window, row_start, across):
    blocks = []
    for member in range(RUN):
        spots, rows = ((1, touched), (window, 1)) if across else ((touched, 1), (1, window))
        spot = lax.broadcasted_iota(jnp.int32, spots, 1 if across else 0)
        row = lax.broadcasted_iota(jnp.int32, rows, 0 if across else 1)
        target = spot + spot // CHUNK * (CHUNK * (RUN - 1))
        first = first_row(row_start, member) * RUN + member * CHUNK - row_start
        blocks.append((target + first == row).astype(f32).astype(bf16))
    return jnp.concatenate(blocks, axis=1 if across else 0)


def cut_kernel(
    meta_ref, scan_ref, above_ref, packed_ref, own_ref, upper_ref, lower_ref, swap_ref
):
    chunks, _, _, width = packed_ref.shape
    window = own_ref.shape[-1]
    quarters = chunks
    slots = 2 * quarters
    lane, quarter = meta_ref[0], meta_ref[1]
    starts = (
        scan_ref[slots + lane * quarters + quarter],
        scan_ref[slots + (1 - lane) * quarters + quarter],
        above_ref[slots + quarter],
        above_ref[slots + quarters + quarter],
    )
    pick = jnp.concatenate([one_hot_down(width, window, start) for start in starts], axis=1)
    for part in range(2):
        rows = jnp.concatenate([packed_ref[chunk, part, :CHUNK] for chunk in range(chunks)], axis=0)
        columns = dot(rows, pick).astype(bf16)
        for index, target in ((0, own_ref), (2, upper_ref), (3, lower_ref)):
            target[part] = columns[:, index * window : (index + 1) * window]
        for chunk in range(chunks):
            swap_ref[chunk, part] = packed_ref[chunk, part, CHUNK:]
        partner = columns[:, window : 2 * window]
        for pair in range(chunks // 2):
            swap_ref[chunks + pair, part] = jnp.concatenate(
                [partner[(2 * pair + i) * CHUNK : (2 * pair + i + 1) * CHUNK] for i in range(2)], axis=1
            )


def touch_kernel(
    meta_ref, scan_ref, own_ref, swapped_ref, below0_ref, below1_ref, touched_ref
):
    lane, quarter, member = meta_ref[0], meta_ref[1], meta_ref[5]
    height, window = own_ref.shape[1:]
    touched = touched_ref.shape[1]
    row_start = scan_ref[lane * QUARTERS + quarter]
    first = first_row(row_start, member)
    pick = jnp.concatenate(
        [
            one_hot(touched, height, first - lane * height),
            one_hot(touched, height, first - (1 - lane) * height),
            one_hot(touched, height, first - 2 * height),
        ],
        axis=1,
    )
    for part in range(2):
        below = below0_ref[part] + below1_ref[part]
        other = []
        for pair in range(QUARTERS, swapped_ref.shape[0]):
            beside = swapped_ref[pair, part]
            other += [beside[:, :window], beside[:, window:]]
        stack = jnp.concatenate([own_ref[part], *other, below], axis=0)
        touched_ref[part] = dot(pick, stack).astype(bf16)


def full_probe(here_ref, there_ref, meta_ref, mode):
    core, up = meta_ref[2], meta_ref[6]
    count = here_ref.shape[0]
    window = here_ref.shape[-1] // 2

    def rows(part):
        pieces = []
        for row in range(count):
            place = lax.rem(up - row + count, count)
            here, there = here_ref[place, mode, part], there_ref[place, mode, part]
            for piece in (jnp.where(core == 0, here, there), jnp.where(core == 0, there, here)):
                pieces += [piece[:, :window], piece[:, window:]]
        return jnp.concatenate(pieces, axis=0).astype(f32)

    return rows(0), rows(1)


def half_product(source_ref, patch, meta_ref, modes, right):
    up, count = meta_ref[6], source_ref.shape[0]
    window = source_ref.shape[-1] // 2
    exits = []
    for mode in modes:
        probe = []
        for part in range(2):
            pieces = []
            for row in range(count):
                piece = source_ref[lax.rem(up - row + count, count), mode, part]
                pieces += [piece[:, :window], piece[:, window:]]
            probe.append(jnp.concatenate(pieces, axis=0).astype(f32))
        exit_real = (probe[0] * patch[0] - probe[1] * patch[1]).astype(bf16)
        exit_imag = (probe[0] * patch[1] + probe[1] * patch[0]).astype(bf16)
        exits.append(jnp.concatenate([exit_real, exit_imag], axis=1))
    return dot(jnp.concatenate(exits, axis=0), right).astype(bf16)


def begin_kernel(meta_ref, scan_ref, touched_ref, here_ref, right_ref, half_ref, patch_ref):
    lane, quarter, core = meta_ref[0], meta_ref[1], meta_ref[2]
    window = touched_ref.shape[-1]
    run = window // (2 * here_ref.shape[0])
    row_start = scan_ref[lane * QUARTERS + quarter]
    pick = class_rows(touched_ref.shape[2], window, row_start, True)
    patch = []
    for part in range(2):
        stack = jnp.concatenate([touched_ref[member, part] for member in range(RUN)], axis=0)
        full = dot(pick, stack)
        even, odd = (
            jnp.concatenate([full[i : i + run] for i in range(first, window, 2 * run)], axis=0)
            for first in (0, run)
        )
        patch.append(jnp.where(core == 0, even, odd))
        patch_ref[part] = jnp.where(core == 0, odd, even)
    rows = half_ref.shape[1]
    modes = range(half_ref.shape[0])
    half = half_product(here_ref, patch, meta_ref, modes, right_ref[...])
    for mode in modes:
        half_ref[mode] = half[mode * rows : (mode + 1) * rows]


def forward_kernel(
    meta_ref, half_ref, patch_ref, there_ref, right_ref, left_ref, spec_ref, power_ref
):
    core = meta_ref[2]
    window = power_ref.shape[-1]
    rows = half_ref.shape[1]
    run = window // (2 * there_ref.shape[0])
    patch = [patch_ref[part] for part in range(2)]
    total = jnp.zeros((window, window), f32)
    for start in range(0, spec_ref.shape[0], AT_ONCE):
        modes = range(start, start + AT_ONCE)
        others = half_product(there_ref, patch, meta_ref, modes, right_ref[...])
        stacks = []
        for i in range(AT_ONCE):
            here, there = half_ref[start + i], others[i * rows : (i + 1) * rows]
            even, odd = jnp.where(core == 0, here, there), jnp.where(core == 0, there, here)
            pieces = []
            for first in range(0, rows, run):
                pieces += [even[first : first + run], odd[first : first + run]]
            stacks.append(on_top(jnp.concatenate(pieces, axis=0)))
        spectra = dot(left_ref[...], jnp.concatenate(stacks, axis=1))
        for i in range(AT_ONCE):
            spectrum = spectra[:, i * window : (i + 1) * window]
            spec_ref[start + i] = spectrum
            squares = spectrum * spectrum
            total = total + (squares[:window] + squares[window:])
    power_ref[...] = total.astype(bf16)


def backward_kernel(
    meta_ref, scan_ref, spec_ref, powers_ref, amplitude_ref, here_ref, there_ref, right_ref, left_ref,
    pieces_ref,
):
    slot = meta_ref[0] * QUARTERS + meta_ref[1]
    alive = slot < scan_ref[4 * QUARTERS + meta_ref[3]]
    window = pieces_ref.shape[-1]
    intensity = powers_ref[0].astype(f32)
    for member in range(1, powers_ref.shape[0]):
        intensity = intensity + powers_ref[member].astype(f32)
    correction = 1.0 - amplitude_ref[0, slot] / jnp.sqrt(intensity + 1.0)
    factor = jnp.where(alive, correction, 0.0)
    sums = [jnp.zeros((window, window), f32)] * 2
    for start in range(0, spec_ref.shape[0], AT_ONCE):
        waves = []
        for mode in range(start, start + AT_ONCE):
            wave_real = (spec_ref[mode, :window] * factor).astype(bf16)
            wave_imag = (spec_ref[mode, window:] * factor).astype(bf16)
            waves.append(jnp.concatenate([wave_real, wave_imag], axis=1))
        back_half = dot(jnp.concatenate(waves, axis=0), left_ref[...]).astype(bf16)
        stacks = [on_top(back_half[i * window : (i + 1) * window]) for i in range(AT_ONCE)]
        back_waves = dot(right_ref[...], jnp.concatenate(stacks, axis=1))
        for i in range(AT_ONCE):
            back_wave = back_waves[:, i * window : (i + 1) * window]
            back_real, back_imag = back_wave[:window], back_wave[window:]
            probe_real, probe_imag = full_probe(here_ref, there_ref, meta_ref, start + i)
            sums[0] = sums[0] + (probe_real * back_real + probe_imag * back_imag)
            sums[1] = sums[1] + (probe_real * back_imag - probe_imag * back_real)
    touched = pieces_ref.shape[2]
    deal = class_rows(touched, window, scan_ref[slot], False)
    for part in range(2):
        dealt = dot(deal, sums[part].astype(bf16)).astype(bf16)
        for member in range(RUN):
            pieces_ref[member, part] = dealt[member * touched : (member + 1) * touched]


def place_kernel(
    meta_ref, scan_ref, above_ref, own_ref, partner_ref, upper_ref, lower_ref, half_ref
):
    chunks, _, chunk_rows, width = half_ref.shape
    height = chunks * chunk_rows
    _, touched, window = own_ref.shape
    quarters = chunks
    slots = 2 * quarters
    lane, quarter, member = meta_ref[0], meta_ref[1], meta_ref[5]
    mine, partners = lane * quarters + quarter, (1 - lane) * quarters + quarter
    first, second = quarter, quarters + quarter
    row_starts = (
        first_row(scan_ref[mine], member) - lane * height,
        first_row(scan_ref[partners], member) - lane * height,
        first_row(above_ref[first], member) - 2 * height,
        first_row(above_ref[second], member) - 2 * height,
    )
    col_starts = (
        scan_ref[slots + mine], scan_ref[slots + partners], above_ref[slots + first], above_ref[slots + second]
    )
    spread = jnp.concatenate([one_hot(window, width, start) for start in col_starts], axis=0)
    sources = (own_ref, partner_ref, upper_ref, lower_ref)
    shifts = [one_hot_down(height, touched, start) for start in row_starts]
    for part in range(2):
        moved = [dot(shift, source[part]).astype(bf16) for shift, source in zip(shifts, sources)]
        placed = dot(jnp.concatenate(moved, axis=1), spread).astype(bf16)
        for chunk in range(chunks):
            half_ref[chunk, part] = placed[chunk * chunk_rows : (chunk + 1) * chunk_rows]


def call(kernel, name, scalars, operands, results, away=(), away_results=(), scratch=(), flops=0):
    held, far = pl.BlockSpec(memory_space=pltpu.VMEM), pl.BlockSpec(memory_space=pltpu.HBM)
    out_specs = held
    if isinstance(results, list):
        out_specs = [far if i in away_results else held for i in range(len(results))]
    return pl.pallas_call(
        kernel,
        grid_spec=pltpu.PrefetchScalarGridSpec(
            num_scalar_prefetch=len(scalars),
            grid=(1,),
            in_specs=[far if i in away else held for i in range(len(operands))],
            out_specs=out_specs,
            scratch_shapes=scratch,
        ),
        out_shape=results,
        compiler_params=pltpu.CompilerParams(vmem_limit_bytes=VMEM_LIMIT),
        cost_estimate=pl.CostEstimate(
            flops=flops, bytes_accessed=4 * 1024 * 1024, transcendentals=0
        ),
        name=name,
    )(*scalars, *operands)


def on_device(
    object_field, probe_modes, measured_amplitude, row_offsets, col_offsets, position_counts
):
    window = probe_modes.shape[-1]
    slots = row_offsets.shape[1]
    width = object_field.shape[2]
    chunk_rows = object_field.shape[1]
    quarters = lax.axis_size("zq")
    tiles = lax.axis_size(TILE_AXES)
    lane, quarter, core = lax.axis_index("xl"), lax.axis_index("zq"), lax.axis_index("c")
    right, left = (jnp.asarray(table) for table in dft_blocks(window))
    swap = [(0, 1), (1, 0)]
    axes = TILE_AXES + ("xl",)
    up_first = [(2 * (t + 1), 2 * t) for t in range(tiles - 1)]
    up_second = [(2 * (t + 1), 2 * t + 1) for t in range(tiles - 1)]
    down_first = [(2 * t, 2 * (t + 1)) for t in range(tiles - 1)]
    down_second = [(2 * t + 1, 2 * (t + 1)) for t in range(tiles - 1)]
    downwards = [(t, t + 1) for t in range(tiles - 1)]

    up = lax.axis_index("y")
    member, tile = lax.axis_index("zr"), lax.axis_index(TILE_AXES)
    meta = jnp.stack([lane, quarter, core, tile, up * 2 + core, member, up]).astype(jnp.int32)
    scan = jnp.concatenate([row_offsets[0], col_offsets[0], position_counts])
    above = lax.ppermute(scan, TILE_AXES, downwards)

    ups = lax.axis_size("y")
    piece_rows = 2 * chunk_rows
    piece = lax.dynamic_slice_in_dim(probe_modes[0], (up * 2 + core) * piece_rows, piece_rows, axis=1)
    piece = jnp.concatenate([piece[:, :chunk_rows], piece[:, chunk_rows:]], axis=2)
    packed = jnp.concatenate([object_field, piece], axis=1).astype(bf16)
    packed = jnp.broadcast_to(packed[None], (quarters,) + packed.shape)
    packed = lax.all_to_all(packed, "zq", 0, 0, tiled=True)
    cut_shape = (2, quarters * chunk_rows, window)
    lane_shape = (quarters, 2, chunk_rows, width)
    own, upper, lower, to_swap = call(
        cut_kernel, "cut", (meta, scan, above), (packed,),
        [jax.ShapeDtypeStruct(cut_shape, bf16)] * 3
        + [jax.ShapeDtypeStruct((quarters + quarters // 2,) + lane_shape[1:], bf16)],
    )
    swapped = lax.ppermute(to_swap, "xl", swap)
    below0 = lax.ppermute(upper, axes, up_first)
    below1 = lax.ppermute(lower, axes, up_second)
    to_swap, swapped, below0, below1 = lax.optimization_barrier((to_swap, swapped, below0, below1))
    lane_modes, other_modes = to_swap[:quarters], swapped[:quarters]
    part_modes = jnp.concatenate([lane_modes, other_modes], axis=0)
    shared = [
        lax.ppermute(part_modes, "y", [(i, (i + d) % ups) for i in range(ups)]) for d in range(1, ups)
    ]
    touched_shape = (2, window // RUN + CHUNK, window)
    touched = call(
        touch_kernel, "touch", (meta, scan), (own, swapped, below0, below1),
        jax.ShapeDtypeStruct(touched_shape, bf16),
    )
    touched = lax.all_gather(touched, "zr", axis=0)
    *shared, touched = lax.optimization_barrier((*shared, touched))
    here = jnp.stack([part_modes, *shared])
    there = lax.ppermute(here, "c", swap)
    modes = here.shape[1]
    product_flops = modes * 2 * 2 * (2 * window) ** 2 * window
    half_spectra, other_patch = call(
        begin_kernel, "begin", (meta, scan), (touched, here, right),
        [
            jax.ShapeDtypeStruct((modes, window // 2, 2 * window), bf16),
            jax.ShapeDtypeStruct((2, window // 2, window), f32),
        ],
        flops=product_flops // 4,
    )
    spectrum, power = call(
        forward_kernel, "forward", (meta,), (half_spectra, other_patch, there, right, left),
        [
            jax.ShapeDtypeStruct((modes, 2 * window, window), f32),
            jax.ShapeDtypeStruct((window, window), bf16),
        ],
        flops=product_flops * 3 // 4,
    )
    powers = lax.all_gather(power, "zr", axis=0)
    pieces = call(
        backward_kernel, "backward", (meta, scan),
        (spectrum, powers, measured_amplitude, here, there, right, left),
        jax.ShapeDtypeStruct(touched.shape, bf16),
        flops=product_flops,
    )
    pieces = lax.all_to_all(pieces, "zr", 0, 0, tiled=True)
    first, second, third, fourth = (pieces[sender].astype(f32) for sender in range(RUN))
    term = ((first + second) + (third + fourth)).astype(bf16)
    partners = lax.ppermute(term, "xl", swap)
    above0 = lax.ppermute(term, axes, down_first)
    above1 = lax.ppermute(term, axes, down_second)
    half_sum = call(
        place_kernel, "place", (meta, scan, above), (term, partners, above0, above1),
        jax.ShapeDtypeStruct(lane_shape, bf16),
    )
    terms = lax.all_to_all(half_sum, "zq", 0, 0, tiled=True)
    return object_field - step_size * jnp.sum(terms.astype(f32), axis=0)


def solution(mesh):
    tiles, modes = mesh.devices.shape
    parts = Mesh(
        mesh.devices.reshape(tiles // 4, 2, 2, 2, 4, modes // 8), TILE_AXES + ("xl",) + DEPTH_AXES
    )
    tile, mode = TILE_AXES, ("xl",) + DEPTH_AXES
    placed = (
        P(None, tile + mode, None),
        P(mode, None, None, None),
        P(tile, None, None, None),
        P(tile, None),
        P(tile, None),
        P(),
    )
    return jax.shard_map(
        on_device,
        mesh=parts,
        in_specs=placed,
        out_specs=P(None, tile + mode, None),
        check_vma=False,
    )
```
